512 devices in a mesh: tm: 16 (over y, x), chan: 32 (over z, core).
Axes of the slice: x: 4, y: 4, z: 16, core: 2. Of those that a mesh axis runs over, the one named last changes fastest.
Arguments:
- records: bfloat16 [128, 1024, 4096], P('tm', None, 'chan'), may hold values from -6 to 6
- pair_list: int32 [2, 32768], P(None, 'chan'), may hold values from 0 to 4095, as said below
- live_count: int32 [32], P('chan'), may hold values from 256 to 1024
Outputs:
- stacks: float32 [2, 256, 32768], P(None, 'tm', 'chan')
The draws below stay inside these ranges and needn't reach their ends.
Inputs may be any that keep to these rules, and one draw needn't show every extreme that they name: pair_list[0, p] lies in channel block p // 1024 (block b holds channels b * 128 to (b + 1) * 128 - 1); pair_list[1, p] lies in a block at most 1 block from it.
All inputs are finite; a program needn't handle non-finite values.
Results may differ from the reference program's by a relative error of at most 0.0047.
Values may be sent and summed in bfloat16 or wider, within the bound.
A program may use at most 64 MiB of HBM per device.

```python
import math
import jax
import jax.numpy as jnp
from jax import lax

SAMPLES = 1024
NF = 256
BAND_LO = 16
REACH = 1
CH_DEV = 128
PAIR_DEV = 1024
CHANNELS = 4096
SEGMENTS = 128
PAIRS = 32768


def draw_pair_list(key, part):
    key = jax.random.fold_in(key, 1)
    blocks = CHANNELS // CH_DEV
    first_key, second_key, third_key = jax.random.split(key, 3)
    owners = jnp.arange(PAIRS, dtype=jnp.int32) // PAIR_DEV
    left_index = owners * CH_DEV + jax.random.randint(first_key, (PAIRS,), 0, CH_DEV, dtype=jnp.int32)
    offsets = jax.random.randint(second_key, (PAIRS,), -REACH, REACH + 1, dtype=jnp.int32)
    target = jnp.clip(owners + offsets, 0, blocks - 1)
    right_index = target * CH_DEV + jax.random.randint(third_key, (PAIRS,), 0, CH_DEV, dtype=jnp.int32)
    left_index = left_index.at[0].set(0)
    right_index = right_index.at[PAIRS - 1].set(CHANNELS - 1)
    return jnp.stack([left_index, right_index]).astype(jnp.int32)


def draw_live_count(key, part):
    key = jax.random.fold_in(key, 2)
    blocks = CHANNELS // CH_DEV
    first_key, second_key = jax.random.split(key, 2)
    counts = jax.random.randint(first_key, (blocks,), PAIR_DEV // 4, PAIR_DEV + 1, dtype=jnp.int32)
    chosen = jax.random.randint(second_key, (), 0, blocks, dtype=jnp.int32)
    counts = counts.at[chosen].set(PAIR_DEV)
    counts = counts.at[(chosen + 1) % blocks].set(PAIR_DEV // 4)
    return counts.astype(jnp.int32)


def block_scale(stream_key, shape, pieces, smallest, high):
    loudness, own = 1.0, jax.random.fold_in(stream_key, 6)
    for dim, parts in pieces:
        steps = jnp.exp(jax.random.uniform(jax.random.fold_in(own, dim), (parts,), jnp.float32, smallest / len(pieces), high / len(pieces)))
        loudness = loudness * jnp.repeat(steps, shape[dim] // parts).reshape([-1 if axis == dim else 1 for axis in range(len(shape))])
    return loudness


def scatter_about(stream_key, extent, spread, most, cuts=(), kind=jnp.bfloat16):
    level = block_scale(stream_key, extent, cuts, -0.22, 0.18) if cuts else 1.0
    values = jax.random.normal(stream_key, extent, jnp.float32) * spread * level
    return jnp.minimum(jnp.maximum(values, -most), most).astype(kind)


def setup_inputs(seed: int = 0) -> dict:
    keys = jax.random.split(jax.random.key(seed), 4)
    records = scatter_about(keys[0], (SEGMENTS, SAMPLES, CHANNELS), 1.0, 6.0, ((0, 16), (2, 32)))
    pair_list = draw_pair_list(jax.random.fold_in(keys[3], 71), 0)
    live_count = draw_live_count(jax.random.fold_in(keys[3], 71), 0)
    return dict(records=records, pair_list=pair_list, live_count=live_count)


EPSILON = 1e-06

def fourier_table(samples, band_bins, lowest):
    sample_ids = jnp.arange(samples, dtype=jnp.int32)
    bin_ids = jnp.arange(band_bins, dtype=jnp.int32) + lowest
    phases = bin_ids[:, None] * sample_ids[None, :] % samples
    angles = phases.astype(jnp.float32) * (2.0 * math.pi / samples)
    tapers = 0.5 - 0.5 * jnp.cos(sample_ids.astype(jnp.float32) * (2.0 * math.pi / samples))
    real_part = jnp.cos(angles) * tapers[None, :]
    imag_part = -jnp.sin(angles) * tapers[None, :]
    return jnp.concatenate([real_part, imag_part], axis=0).astype(jnp.bfloat16)

def reference(records, pair_list, live_count):
    basis_wide = fourier_table(SAMPLES, NF, BAND_LO).astype(jnp.float32)
    left_index = pair_list[0]
    right_index = pair_list[1]

    def accumulate(running, segment):
        spectrum = jnp.dot(basis_wide, segment.astype(jnp.float32), precision=lax.Precision.HIGHEST)
        powers = lax.optimization_barrier(jnp.sum(spectrum * spectrum, axis=0)) / NF
        whitened = (spectrum * lax.rsqrt(powers + EPSILON)[None, :]).astype(jnp.bfloat16)
        whitened = whitened.reshape(2, NF, CHANNELS)
        left_part = jnp.take(whitened, left_index, axis=2).astype(jnp.float32)
        right_part = jnp.take(whitened, right_index, axis=2).astype(jnp.float32)
        real_part = left_part[0] * right_part[0] + left_part[1] * right_part[1]
        imag_part = left_part[1] * right_part[0] - left_part[0] * right_part[1]
        return (running + jnp.stack([real_part, imag_part]), None)
    initial = jnp.zeros((2, NF, PAIRS), jnp.float32)
    totals, unused = lax.scan(accumulate, initial, records)
    slot_ids = jnp.arange(PAIRS, dtype=jnp.int32) % PAIR_DEV
    slot_mask = (slot_ids < jnp.repeat(live_count, PAIR_DEV)).astype(jnp.float32)
    return totals / SEGMENTS * slot_mask[None, None, :]
```

```python
import math

import jax
import jax.numpy as jnp
import ml_dtypes
import numpy as np
from jax import lax
from jax.experimental import pallas as pl
from jax.experimental.pallas import tpu as pltpu
from jax.sharding import PartitionSpec as P

SAMPLES = 1024
NF = 256
BAND_LO = 16
EPSILON = 1e-06

SIDE = 4
SEG = 8
CH = 128
PAIRS = 1024
CHUNKS = 8
ROWS = 2 * NF // CHUNKS
TILE = 256
TILES = PAIRS // TILE
MESH = pl.DeviceIdType.MESH


def basis_rows():
    sample_ids = np.arange(SAMPLES, dtype=np.int64)
    bin_ids = np.arange(NF, dtype=np.int64) + BAND_LO
    phases = bin_ids[:, None] * sample_ids[None, :] % SAMPLES
    step = np.float32(2.0 * math.pi / SAMPLES)
    angles = phases.astype(np.float32) * step
    tapers = np.float32(0.5) - np.float32(0.5) * np.cos(sample_ids.astype(np.float32) * step)
    table = np.stack([np.cos(angles) * tapers[None, :], -np.sin(angles) * tapers[None, :]])
    table = table.reshape(2, SIDE, SIDE, CHUNKS, 2, SAMPLES)
    parts = []
    for k in range(CHUNKS):
        part = table[:, :, :, k]
        if k % 2 == 0:
            part = part.transpose(0, 2, 1, 3, 4)
        parts.append(part.reshape(ROWS, SAMPLES))
    return np.concatenate(parts, axis=0).astype(np.float32).astype(ml_dtypes.bfloat16)


def kernel(
    basis_hbm, rec_hbm, pair_hbm, live_hbm, out_ref,
    basis, rec, pair, live, own, low, high, w_left, w_right,
    part, send1, recv1, part2, send2, recv2,
    in_sem, z_send, z_recv, p1_send, p1_recv, p2_send, p2_recv,
):
    t = lax.axis_index("tm")
    c = lax.axis_index("chan")
    n_chan = lax.axis_size("chan")
    y, x = lax.div(t, SIDE), lax.rem(t, SIDE)
    c_high = lax.rem(c + 1, n_chan)
    c_low = lax.rem(c + n_chan - 1, n_chan)

    pair_copy = pltpu.make_async_copy(pair_hbm, pair, in_sem.at[0])
    live_copy = pltpu.make_async_copy(live_hbm, live, in_sem.at[1])
    basis_copy = pltpu.make_async_copy(basis_hbm, basis, in_sem.at[2])
    rec_copies = [
        pltpu.make_async_copy(rec_hbm.at[pl.ds(2 * q, 2)], rec.at[pl.ds(2 * q, 2)], in_sem.at[3 + q])
        for q in range(SEG // 2)
    ]
    rec_copies[0].start()
    basis_copy.start()
    for q in range(1, SEG // 2):
        rec_copies[q].start()
    pair_copy.start()
    live_copy.start()

    def x_peer(d):
        return y * SIDE + lax.rem(x + d, SIDE)

    def y_peer(d):
        return lax.rem(y + d, SIDE) * SIDE + x

    barrier = pltpu.get_barrier_semaphore()
    for peer in (c_low, c_high):
        pl.semaphore_signal(barrier, inc=1, device_id=(t, peer), device_id_type=MESH)
    for d in range(1, SIDE):
        pl.semaphore_signal(barrier, inc=1, device_id=(x_peer(d), c), device_id_type=MESH)
        pl.semaphore_signal(barrier, inc=1, device_id=(y_peer(d), c), device_id_type=MESH)

    def z_copies(k, q):
        if q is None:
            piece, sem = (k,), k + 3
        else:
            piece, sem = (k, pl.ds(2 * q, 2)), q
        return [
            pltpu.make_async_remote_copy(
                src_ref=own.at[piece],
                dst_ref=landing.at[piece],
                send_sem=z_send.at[way, sem],
                recv_sem=z_recv.at[way, sem],
                device_id=(t, peer),
                device_id_type=MESH,
            )
            for way, landing, peer in ((0, high, c_low), (1, low, c_high))
        ]

    z_started = {}
    basis_copy.wait()
    for q in range(SEG // 2):
        rec_copies[q].wait()
        wide = jnp.concatenate([rec[2 * q], rec[2 * q + 1]], axis=1)
        spectrum = jnp.dot(basis[...], wide, preferred_element_type=jnp.float32)
        powers = jnp.sum(spectrum * spectrum, axis=0, keepdims=True) / NF
        white = (spectrum * lax.rsqrt(powers + EPSILON)).astype(jnp.bfloat16)
        white = white.reshape(CHUNKS, ROWS, 2 * CH)
        own[:, 2 * q] = white[:, :, :CH]
        own[:, 2 * q + 1] = white[:, :, CH:]
        if q == 0:
            pl.semaphore_wait(barrier, 2 + 2 * (SIDE - 1))
        z_started[0, q] = z_copies(0, q)
        for copy in z_started[0, q]:
            copy.start()
    for k in range(1, CHUNKS):
        z_started[k, None] = z_copies(k, None)
        for copy in z_started[k, None]:
            copy.start()

    pair_copy.wait()
    live_copy.wait()
    n_live = live[0]
    for n in range(TILES):
        cols = pl.ds(n * TILE, TILE)
        left = pair[0:1, cols] - c * CH
        right = pair[1:2, cols] - (c - 1) * CH
        slots = lax.broadcasted_iota(jnp.int32, (1, TILE), 1) + n * TILE
        left = jnp.where(slots < n_live, left, -1)
        ids = lax.broadcasted_iota(jnp.int32, (CH, TILE), 0)
        w_left[n] = jnp.where(ids == left, 1.0 / 128.0, 0.0).astype(jnp.bfloat16)
        for place, block in ((0, 1), (1, 0), (2, 2)):
            hot = jnp.where(ids + block * CH == right, 1.0, 0.0)
            w_right[n, pl.ds(place * CH, CH)] = hot.astype(jnp.bfloat16)

    half = ROWS // 2
    group = half // SIDE

    def multiply(k):
        def step(n, carry):
            mine = own[k].reshape(SEG * ROWS, CH)
            wide = jnp.concatenate(
                [mine, low[k].reshape(SEG * ROWS, CH), high[k].reshape(SEG * ROWS, CH)], axis=1
            )
            left = jnp.dot(mine, w_left[n], preferred_element_type=jnp.float32)
            right = jnp.dot(wide, w_right[n], preferred_element_type=jnp.float32)
            left = left.reshape(SEG, 2, half, TILE)
            right = right.reshape(SEG, 2, half, TILE)
            real = jnp.sum(left[:, 0] * right[:, 0] + left[:, 1] * right[:, 1], axis=0)
            imag = jnp.sum(left[:, 1] * right[:, 0] - left[:, 0] * right[:, 1], axis=0)
            cols = pl.ds(pl.multiple_of(n * TILE, TILE), TILE)
            for a in range(SIDE):
                rows = slice(a * group, (a + 1) * group)
                both = jnp.concatenate([real[rows], imag[rows]], axis=0)
                part[k % 2, a, :, cols] = both
                send1[k, a, :, cols] = both.astype(jnp.bfloat16)
            return carry

        lax.fori_loop(0, TILES, step, 0)

    def first(k):
        return (x, x_peer) if k % 2 == 0 else (y, y_peer)

    def second(k):
        return (y, y_peer) if k % 2 == 0 else (x, x_peer)

    def exchange(k, phase):
        place, peer = first(k) if phase == 1 else second(k)
        source, landing = (send1, recv1) if phase == 1 else (send2, recv2)
        sends, recvs = (p1_send, p1_recv) if phase == 1 else (p2_send, p2_recv)
        copies = [
            pltpu.make_async_remote_copy(
                src_ref=source.at[k, lax.rem(place + d, SIDE)],
                dst_ref=landing.at[k, d - 1],
                send_sem=sends.at[k, d - 1],
                recv_sem=recvs.at[k, d - 1],
                device_id=(peer(d), c),
                device_id_type=MESH,
            )
            for d in (2, 1, 3)
        ]
        for copy in copies:
            copy.start()
        return copies

    def add_first(k):
        place, _ = first(k)
        total = part[k % 2, place]
        for d in range(SIDE - 1):
            total = total + recv1[k, d].astype(jnp.float32)
        for b in range(SIDE):
            pieces = []
            for g in range(TILES):
                cols = slice(g * TILE, (g + 1) * TILE)
                pieces.append(total[2 * b:2 * b + 2, cols])
                pieces.append(total[group + 2 * b:group + 2 * b + 2, cols])
            both = jnp.concatenate(pieces, axis=0)
            part2[k % 2, b] = both
            send2[k, b] = both.astype(jnp.bfloat16)

    def add_second(k):
        place, _ = second(k)
        total = part2[k % 2, place]
        for d in range(SIDE - 1):
            total = total + recv2[k, d].astype(jnp.float32)
        for g in range(TILES):
            cols = pl.ds(g * TILE, TILE)
            out_ref[0, 2 * k:2 * k + 2, cols] = total[4 * g:4 * g + 2]
            out_ref[1, 2 * k:2 * k + 2, cols] = total[4 * g + 2:4 * g + 4]

    phase1, phase2 = {}, {}

    def finish_first(k):
        for copy in phase1[k]:
            copy.wait()
        add_first(k)
        phase2[k] = exchange(k, 2)

    def finish_second(k):
        for copy in phase2[k]:
            copy.wait()
        add_second(k)

    for k in range(CHUNKS):
        for copies in [z_started[key] for key in z_started if key[0] == k]:
            for copy in copies:
                copy.wait()
        multiply(k)
        phase1[k] = exchange(k, 1)
        if k >= 1:
            finish_first(k - 1)
        if k >= 2:
            finish_second(k - 2)
    finish_first(CHUNKS - 1)
    finish_second(CHUNKS - 2)
    finish_second(CHUNKS - 1)


def body(records, pair_list, live_count):
    table = jnp.asarray(basis_rows())
    any_space = pl.BlockSpec(memory_space=pl.ANY)
    vmem, bf16, f32 = pltpu.VMEM, jnp.bfloat16, jnp.float32
    dma = pltpu.SemaphoreType.DMA
    group = ROWS // SIDE
    return pl.pallas_call(
        kernel,
        out_shape=jax.ShapeDtypeStruct((2, 2 * CHUNKS, PAIRS), f32),
        in_specs=[any_space] * 4,
        out_specs=pl.BlockSpec(memory_space=vmem),
        scratch_shapes=[
            vmem((2 * NF, SAMPLES), bf16),
            vmem((SEG, SAMPLES, CH), bf16),
            vmem((2, PAIRS), jnp.int32),
            pltpu.SMEM((1,), jnp.int32),
            vmem((CHUNKS, SEG, ROWS, CH), bf16),
            vmem((CHUNKS, SEG, ROWS, CH), bf16),
            vmem((CHUNKS, SEG, ROWS, CH), bf16),
            vmem((TILES, CH, TILE), bf16),
            vmem((TILES, 3 * CH, TILE), bf16),
            vmem((2, SIDE, group, PAIRS), f32),
            vmem((CHUNKS, SIDE, group, PAIRS), bf16),
            vmem((CHUNKS, SIDE - 1, group, PAIRS), bf16),
            vmem((2, SIDE, group, TILE), f32),
            vmem((CHUNKS, SIDE, group, TILE), bf16),
            vmem((CHUNKS, SIDE - 1, group, TILE), bf16),
            dma((3 + SEG // 2,)),
            dma((2, CHUNKS + 3)),
            dma((2, CHUNKS + 3)),
            dma((CHUNKS, SIDE - 1)),
            dma((CHUNKS, SIDE - 1)),
            dma((CHUNKS, SIDE - 1)),
            dma((CHUNKS, SIDE - 1)),
        ],
        compiler_params=pltpu.CompilerParams(
            collective_id=0, has_side_effects=True, vmem_limit_bytes=56 * 2**20
        ),
        cost_estimate=pl.CostEstimate(
            flops=7 * 10**9, bytes_accessed=4 * 2**20, transcendentals=0
        ),
    )(table, records, pair_list, live_count)


def solution(mesh):
    in_specs = (P("tm", None, "chan"), P(None, "chan"), P("chan"))
    out_specs = P(None, "tm", "chan")
    return jax.shard_map(body, mesh=mesh, in_specs=in_specs, out_specs=out_specs, check_vma=False)
```

```python
import math

import jax
import jax.numpy as jnp
import ml_dtypes
import numpy as np
from jax import lax
from jax.experimental import pallas as pl
from jax.experimental.pallas import tpu as pltpu
from jax.sharding import PartitionSpec as P

SAMPLES = 1024
NF = 256
BAND_LO = 16
EPSILON = 1e-06

SIDE = 4
OWNERS = SIDE * SIDE
SEG = 8
CH = 128
PAIRS = 1024
BINS = 8
ROWS = 2 * BINS
TILE = 256
TILES = PAIRS // TILE
QUADS = SEG // 2
MESH = pl.DeviceIdType.MESH


def basis_tables():
    sample_ids = np.arange(SAMPLES, dtype=np.int64)
    bin_ids = np.arange(NF, dtype=np.int64) + BAND_LO
    phases = bin_ids[:, None] * sample_ids[None, :] % SAMPLES
    step = np.float32(2.0 * math.pi / SAMPLES)
    angles = phases.astype(np.float32) * step
    tapers = np.float32(0.5) - np.float32(0.5) * np.cos(sample_ids.astype(np.float32) * step)
    table = np.stack([np.cos(angles) * tapers[None, :], -np.sin(angles) * tapers[None, :]])
    table = table.astype(np.float32).astype(ml_dtypes.bfloat16)
    table = table.reshape(2, SIDE, SIDE, 2, BINS, SAMPLES).transpose(3, 1, 2, 0, 4, 5)
    table = table.reshape(2, SIDE, SIDE, ROWS, SAMPLES)
    ids = np.arange(2 * SIDE - 1) % SIDE
    first = table[0][ids[None, :], (ids[:, None] + ids[None, :]) % SIDE]
    second = table[1][ids[:, None], ids[None, :]]
    return first, second


def kernel(
    basis_a_hbm, basis_b_hbm, rec_hbm, pair_hbm, live_hbm, out_ref,
    basis, rec, pair, live, w_left, w_right,
    own_a, low_a, high_a, stage_b, own_b, low_b, high_b, own_sum, send_sum, recv_sum, total_b,
    in_sem, za_send, za_recv, zb_send, zb_recv, gather_send, gather_recv, sum_send, sum_recv,
):
    t = lax.axis_index("tm")
    c = lax.axis_index("chan")
    n_chan = lax.axis_size("chan")
    y, x = lax.div(t, SIDE), lax.rem(t, SIDE)
    c_high = lax.rem(c + 1, n_chan)
    c_low = lax.rem(c + n_chan - 1, n_chan)
    ways = ((0, high_a, high_b, c_low), (1, low_a, low_b, c_high))

    def peer(dy, dx):
        return (lax.rem(y + dy, SIDE) * SIDE + lax.rem(x + dx, SIDE), c)

    others = [(dy, dx) for dy in (2, 1, 3, 0) for dx in (2, 1, 3, 0) if (dy, dx) != (0, 0)]

    skew = lax.rem(x - y + SIDE, SIDE)
    basis_copies = [
        pltpu.make_async_copy(table.at[pl.ds(u, SIDE), pl.ds(v, SIDE)], basis.at[h], in_sem.at[2 + h])
        for h, (table, u, v) in enumerate(((basis_a_hbm, skew, y), (basis_b_hbm, y, x)))
    ]
    rec_copies = [
        pltpu.make_async_copy(rec_hbm.at[pl.ds(2 * q, 2)], rec.at[pl.ds(2 * q, 2)], in_sem.at[4 + q])
        for q in range(QUADS)
    ]
    pair_copy = pltpu.make_async_copy(pair_hbm, pair, in_sem.at[0])
    live_copy = pltpu.make_async_copy(live_hbm, live, in_sem.at[1])
    rec_copies[0].start()
    for copy in basis_copies:
        copy.start()
    for q in range(1, QUADS):
        rec_copies[q].start()
    pair_copy.start()
    live_copy.start()

    barrier = pltpu.get_barrier_semaphore()
    for to in [(t, c_low), (t, c_high)] + [peer(dy, dx) for dy, dx in others]:
        pl.semaphore_signal(barrier, inc=1, device_id=to, device_id_type=MESH)

    def send(source, landing, send_sem, recv_sem, to):
        copy = pltpu.make_async_remote_copy(
            src_ref=source,
            dst_ref=landing,
            send_sem=send_sem,
            recv_sem=recv_sem,
            device_id=to,
            device_id_type=MESH,
        )
        copy.start()
        return copy

    za, zb = {}, {}
    for copy in basis_copies:
        copy.wait()
    for q in range(QUADS):
        rec_copies[q].wait()
        wide = jnp.concatenate([rec[2 * q], rec[2 * q + 1]], axis=1)
        spectrum = jnp.dot(
            basis[...].reshape(2 * NF, SAMPLES), wide, preferred_element_type=jnp.float32
        )
        powers = jnp.sum(spectrum * spectrum, axis=0, keepdims=True) / NF
        white = (spectrum * lax.rsqrt(powers + EPSILON)).astype(jnp.bfloat16)
        for e in range(2):
            mine = white[:, e * CH:(e + 1) * CH].reshape(2, OWNERS, ROWS, CH)
            own_a[:, :, 2 * q + e] = mine[0].reshape(SIDE, SIDE, ROWS, CH)
            stage_b[q, :, e] = mine[1]
            own_b[q, 0, e] = mine[1, 0]
        if q == 0:
            pl.semaphore_wait(barrier, 2 + len(others))
        piece = (0, pl.ds(0, SIDE), pl.ds(2 * q, 2))
        for way, landing, _, to in ways:
            za[0, q, way] = send(
                own_a.at[piece], landing.at[piece], za_send.at[way, q], za_recv.at[way, q], (t, to)
            )
        for dy, dx in others:
            d = dy * SIDE + dx
            send(
                stage_b.at[q, d], own_b.at[q, d], gather_send.at[q], gather_recv.at[q], peer(dy, dx)
            )
    for k in range(1, SIDE):
        for way, landing, _, to in ways:
            sem = QUADS + k - 1
            za[k, 0, way] = send(
                own_a.at[k], landing.at[k], za_send.at[way, sem], za_recv.at[way, sem], (t, to)
            )

    pair_copy.wait()
    live_copy.wait()
    n_live = live[0]
    for n in range(TILES):
        cols = pl.ds(n * TILE, TILE)
        left = pair[0:1, cols] - c * CH
        right = pair[1:2, cols] - (c - 1) * CH
        slots = lax.broadcasted_iota(jnp.int32, (1, TILE), 1) + n * TILE
        left = jnp.where(slots < n_live, left, -1)
        ids = lax.broadcasted_iota(jnp.int32, (CH, TILE), 0)
        w_left[n] = jnp.where(ids == left, 1.0 / 128.0, 0.0).astype(jnp.bfloat16)
        for place, block in ((0, 1), (1, 0), (2, 2)):
            hot = jnp.where(ids + block * CH == right, 1.0, 0.0)
            w_right[n, pl.ds(place * CH, CH)] = hot.astype(jnp.bfloat16)

    def multiply(own, low, high, groups):
        mine = own.reshape(-1, CH)
        wide = jnp.concatenate([mine, low.reshape(-1, CH), high.reshape(-1, CH)], axis=1)
        shape = (groups, mine.shape[0] // (groups * ROWS), 2, BINS, TILE)
        sums = []
        for n in range(TILES):
            left = jnp.dot(mine, w_left[n], preferred_element_type=jnp.float32).reshape(shape)
            right = jnp.dot(wide, w_right[n], preferred_element_type=jnp.float32).reshape(shape)
            real = jnp.sum(left[:, :, 0] * right[:, :, 0] + left[:, :, 1] * right[:, :, 1], axis=1)
            imag = jnp.sum(left[:, :, 1] * right[:, :, 0] - left[:, :, 0] * right[:, :, 1], axis=1)
            sums.append(jnp.concatenate([real, imag], axis=1))
        return sums

    def tile(n):
        return pl.ds(n * TILE, TILE)

    def part_a(k):
        for key in za:
            if key[0] == k:
                za[key].wait()
        for n, both in enumerate(multiply(own_a[k], low_a[k], high_a[k], SIDE)):
            if k == 0:
                own_sum[:, tile(n)] = both[0]
            send_sum[k, :, :, tile(n)] = both.astype(jnp.bfloat16)
        for i in range(SIDE):
            dx = (i + k) % SIDE
            if (i, dx) != (0, 0):
                send(
                    send_sum.at[k, i], recv_sum.at[k, i], sum_send.at[k], sum_recv.at[k], peer(i, dx)
                )

    def wait_bytes(ref, sem):
        pltpu.make_async_copy(ref, ref, sem).wait()

    def forward_b(q):
        wait_bytes(own_b.at[q, pl.ds(1, OWNERS - 1)], gather_recv.at[q])
        for way, _, landing, to in ways:
            zb[q, way] = send(
                own_b.at[q], landing.at[q], zb_send.at[way, q], zb_recv.at[way, q], (t, to)
            )

    def part_b(q):
        for way in range(2):
            zb[q, way].wait()
        for n, both in enumerate(multiply(own_b[q], low_b[q], high_b[q], 1)):
            if q == 0:
                total_b[:, tile(n)] = both[0]
            elif q < QUADS - 1:
                total_b[:, tile(n)] += both[0]
            else:
                total = total_b[:, tile(n)] + both[0]
                out_ref[0, BINS:, tile(n)] = total[:BINS]
                out_ref[1, BINS:, tile(n)] = total[BINS:]

    def add_sums(k):
        lowest = 1 if k == 0 else 0
        wait_bytes(recv_sum.at[k, pl.ds(lowest, SIDE - lowest)], sum_recv.at[k])
        total = own_sum[...]
        for i in range(lowest, SIDE):
            total = total + recv_sum[k, i].astype(jnp.float32)
        if k < SIDE - 1:
            own_sum[...] = total
        else:
            out_ref[0, :BINS] = total[:BINS]
            out_ref[1, :BINS] = total[BINS:]

    for k in range(SIDE):
        part_a(k)
        forward_b(k)
    part_b(0)
    part_b(1)
    add_sums(0)
    add_sums(1)
    part_b(2)
    add_sums(2)
    part_b(3)
    add_sums(3)
    for q in range(QUADS):
        wait_bytes(stage_b.at[q, pl.ds(1, OWNERS - 1)], gather_send.at[q])
    for k in range(SIDE):
        lowest = 1 if k == 0 else 0
        wait_bytes(send_sum.at[k, pl.ds(lowest, SIDE - lowest)], sum_send.at[k])


def body(records, pair_list, live_count):
    tables = [jnp.asarray(table) for table in basis_tables()]
    any_space = pl.BlockSpec(memory_space=pl.ANY)
    vmem, bf16, f32 = pltpu.VMEM, jnp.bfloat16, jnp.float32
    dma = pltpu.SemaphoreType.DMA
    block_a = vmem((SIDE, SIDE, SEG, ROWS, CH), bf16)
    block_b = vmem((QUADS, OWNERS, 2, ROWS, CH), bf16)
    return pl.pallas_call(
        kernel,
        out_shape=jax.ShapeDtypeStruct((2, 2 * BINS, PAIRS), f32),
        in_specs=[any_space] * 5,
        out_specs=pl.BlockSpec(memory_space=vmem),
        scratch_shapes=[
            vmem((2, SIDE, SIDE, ROWS, SAMPLES), bf16),
            vmem((SEG, SAMPLES, CH), bf16),
            vmem((2, PAIRS), jnp.int32),
            pltpu.SMEM((1,), jnp.int32),
            vmem((TILES, CH, TILE), bf16),
            vmem((TILES, 3 * CH, TILE), bf16),
            block_a,
            block_a,
            block_a,
            block_b,
            block_b,
            block_b,
            block_b,
            vmem((ROWS, PAIRS), f32),
            vmem((SIDE, SIDE, ROWS, PAIRS), bf16),
            vmem((SIDE, SIDE, ROWS, PAIRS), bf16),
            vmem((ROWS, PAIRS), f32),
            dma((4 + QUADS,)),
            dma((2, QUADS + SIDE - 1)),
            dma((2, QUADS + SIDE - 1)),
            dma((2, QUADS)),
            dma((2, QUADS)),
            dma((QUADS,)),
            dma((QUADS,)),
            dma((SIDE,)),
            dma((SIDE,)),
        ],
        compiler_params=pltpu.CompilerParams(
            collective_id=0, has_side_effects=True, vmem_limit_bytes=56 * 2**20
        ),
        cost_estimate=pl.CostEstimate(
            flops=7 * 10**9, bytes_accessed=4 * 2**20, transcendentals=0
        ),
    )(*tables, records, pair_list, live_count)


def solution(mesh):
    in_specs = (P("tm", None, "chan"), P(None, "chan"), P("chan"))
    out_specs = P(None, "tm", "chan")
    return jax.shard_map(body, mesh=mesh, in_specs=in_specs, out_specs=out_specs, check_vma=False)
```

```python
import functools
import math

import jax
import jax.numpy as jnp
import ml_dtypes
import numpy as np
from jax import lax
from jax.experimental import pallas as pl
from jax.experimental.pallas import tpu as pltpu
from jax.sharding import PartitionSpec as P

SAMPLES = 1024
NF = 256
BAND_LO = 16
EPSILON = 1e-06

SIDE = 4
OWNERS = SIDE * SIDE
SEG = 8
CH = 128
PAIRS = 1024
BINS = 8
ROWS = 2 * BINS
TILE = 256
TILES = PAIRS // TILE
QUADS = SEG // 2
EARLY = 2
MESH = pl.DeviceIdType.MESH


def basis_tables():
    sample_ids = np.arange(SAMPLES, dtype=np.int64)
    bin_ids = np.arange(NF, dtype=np.int64) + BAND_LO
    phases = bin_ids[:, None] * sample_ids[None, :] % SAMPLES
    step = np.float32(2.0 * math.pi / SAMPLES)
    angles = phases.astype(np.float32) * step
    tapers = np.float32(0.5) - np.float32(0.5) * np.cos(sample_ids.astype(np.float32) * step)
    table = np.stack([np.cos(angles) * tapers[None, :], -np.sin(angles) * tapers[None, :]])
    table = table.astype(np.float32).astype(ml_dtypes.bfloat16)
    table = table.reshape(2, SIDE, SIDE, 2, BINS, SAMPLES).transpose(3, 1, 2, 0, 4, 5)
    table = table.reshape(2, SIDE, SIDE, ROWS, SAMPLES)
    ids = np.arange(2 * SIDE - 1) % SIDE
    first = table[0][ids[None, :], (ids[:, None] + ids[None, :]) % SIDE]
    second = table[1][ids[:, None], ids[None, :]]
    return first, second


def kernel(
    basis_a_hbm, basis_b_hbm, rec_hbm, pair_hbm, live_hbm, out_ref,
    basis, rec, pair, live, w_left, w_right,
    own_a, near_a, far_a, stage_b, own_b, near_b, far_b, own_sum, send_sum, recv_sum, total_b,
    in_sem, za_send, za_recv, zb_send, zb_recv, gather_send, gather_recv, sum_send, sum_recv,
):
    t = lax.axis_index("tm")
    c = lax.axis_index("chan")
    n_chan = lax.axis_size("chan")
    y, x = lax.div(t, SIDE), lax.rem(t, SIDE)
    side = 1 - 2 * lax.rem(c, 2)
    c_near, c_far = c + side, c - side
    has_far = jnp.logical_and(c_far >= 0, c_far < n_chan)
    one_far = jnp.where(has_far, 1, 0)
    ways = ((0, near_a, near_b, c_near), (1, far_a, far_b, c_far))

    def on_way(way, act):
        if way == 0:
            act()
        else:
            pl.when(has_far)(act)

    def peer(dy, dx):
        return (lax.rem(y + dy, SIDE) * SIDE + lax.rem(x + dx, SIDE), c)

    others = [(dy, dx) for dy in (2, 1, 3, 0) for dx in (2, 1, 3, 0) if (dy, dx) != (0, 0)]

    skew = lax.rem(x - y + SIDE, SIDE)
    basis_copies = [
        pltpu.make_async_copy(table.at[pl.ds(u, SIDE), pl.ds(v, SIDE)], basis.at[h], in_sem.at[2 + h])
        for h, (table, u, v) in enumerate(((basis_a_hbm, skew, y), (basis_b_hbm, y, x)))
    ]
    rec_copies = [
        pltpu.make_async_copy(rec_hbm.at[pl.ds(2 * q, 2)], rec.at[pl.ds(2 * q, 2)], in_sem.at[4 + q])
        for q in range(QUADS)
    ]
    pair_copy = pltpu.make_async_copy(pair_hbm, pair, in_sem.at[0])
    live_copy = pltpu.make_async_copy(live_hbm, live, in_sem.at[1])
    rec_copies[0].start()
    for copy in basis_copies:
        copy.start()
    for q in range(1, QUADS):
        rec_copies[q].start()
    pair_copy.start()
    live_copy.start()

    barrier = pltpu.get_barrier_semaphore()
    for to in [(t, c_near)] + [peer(dy, dx) for dy, dx in others]:
        pl.semaphore_signal(barrier, inc=1, device_id=to, device_id_type=MESH)

    @pl.when(has_far)
    def _():
        pl.semaphore_signal(barrier, inc=1, device_id=(t, c_far), device_id_type=MESH)

    @pl.when(jnp.logical_not(has_far))
    def _():
        far_a[...] = jnp.zeros_like(far_a)
        far_b[...] = jnp.zeros_like(far_b)

    def make(source, landing, send_sem, recv_sem, to):
        return pltpu.make_async_remote_copy(
            src_ref=source,
            dst_ref=landing,
            send_sem=send_sem,
            recv_sem=recv_sem,
            device_id=to,
            device_id_type=MESH,
        )

    za, zb = [], []

    def send_z(copies, started=za):
        started.extend(copies)
        for way in (1, 0):
            @functools.partial(on_way, way)
            def _():
                for _, w, copy in copies:
                    if w == way:
                        copy.start()

    def wait_z(k, started=za):
        for way in range(2):
            @functools.partial(on_way, way)
            def _():
                for part, w, copy in started:
                    if part == k and w == way:
                        copy.wait()

    for copy in basis_copies:
        copy.wait()
    for q in range(QUADS):
        rec_copies[q].wait()
        wide = jnp.concatenate([rec[2 * q], rec[2 * q + 1]], axis=1)
        spectrum = jnp.dot(
            basis[...].reshape(2 * NF, SAMPLES), wide, preferred_element_type=jnp.float32
        )
        powers = jnp.sum(spectrum * spectrum, axis=0, keepdims=True) / NF
        white = (spectrum * lax.rsqrt(powers + EPSILON)).astype(jnp.bfloat16)
        for e in range(2):
            mine = white[:, e * CH:(e + 1) * CH].reshape(2, OWNERS, ROWS, CH)
            own_a[:, :, 2 * q + e] = mine[0].reshape(SIDE, SIDE, ROWS, CH)
            stage_b[q, :, e] = mine[1]
            own_b[q, 0, e] = mine[1, 0]
        if q == 0:
            pl.semaphore_wait(barrier, 1 + one_far + len(others))
        for k in range(EARLY):
            piece = (k, pl.ds(0, SIDE), pl.ds(2 * q, 2))
            sem = k * QUADS + q
            send_z([
                (k, way, make(own_a.at[piece], landing.at[piece], za_send.at[way, sem], za_recv.at[way, sem], (t, to)))
                for way, landing, _, to in ways
            ])
        for dy, dx in others:
            d = dy * SIDE + dx
            make(
                stage_b.at[q, d], own_b.at[q, d], gather_send.at[q], gather_recv.at[q], peer(dy, dx)
            ).start()
    for k in range(EARLY, SIDE):
        sem = QUADS * EARLY + k - EARLY
        send_z([
            (k, way, make(own_a.at[k], landing.at[k], za_send.at[way, sem], za_recv.at[way, sem], (t, to)))
            for way, landing, _, to in ways
        ])

    pair_copy.wait()
    live_copy.wait()
    n_live = live[0]
    for n in range(TILES):
        cols = pl.ds(n * TILE, TILE)
        left = pair[0:1, cols] - c * CH
        right = pair[1:2, cols] - (c - 1) * CH
        slots = lax.broadcasted_iota(jnp.int32, (1, TILE), 1) + n * TILE
        left = jnp.where(slots < n_live, left, -1)
        ids = lax.broadcasted_iota(jnp.int32, (CH, TILE), 0)
        w_left[n] = jnp.where(ids == left, 1.0 / 128.0, 0.0).astype(jnp.bfloat16)
        for place, block in ((0, 1), (1, 1 + side), (2, 1 - side)):
            hot = jnp.where(ids + block * CH == right, 1.0, 0.0)
            w_right[n, pl.ds(place * CH, CH)] = hot.astype(jnp.bfloat16)

    def multiply(own, near, far, groups):
        mine = own.reshape(-1, CH)
        wide = jnp.concatenate([mine, near.reshape(-1, CH), far.reshape(-1, CH)], axis=1)
        shape = (groups, mine.shape[0] // (groups * ROWS), 2, BINS, TILE)
        sums = []
        for n in range(TILES):
            left = jnp.dot(mine, w_left[n], preferred_element_type=jnp.float32).reshape(shape)
            right = jnp.dot(wide, w_right[n], preferred_element_type=jnp.float32).reshape(shape)
            real = jnp.sum(left[:, :, 0] * right[:, :, 0] + left[:, :, 1] * right[:, :, 1], axis=1)
            imag = jnp.sum(left[:, :, 1] * right[:, :, 0] - left[:, :, 0] * right[:, :, 1], axis=1)
            sums.append(jnp.concatenate([real, imag], axis=1))
        return sums

    def tile(n):
        return pl.ds(n * TILE, TILE)

    def part_a(k):
        wait_z(k)
        for n, both in enumerate(multiply(own_a[k], near_a[k], far_a[k], SIDE)):
            if k == 0:
                own_sum[:, tile(n)] = both[0]
            send_sum[k, :, :, tile(n)] = both.astype(jnp.bfloat16)
        for i in range(SIDE):
            dx = (i + k) % SIDE
            if (i, dx) != (0, 0):
                make(
                    send_sum.at[k, i], recv_sum.at[k, i], sum_send.at[k], sum_recv.at[k], peer(i, dx)
                ).start()

    def wait_bytes(ref, sem):
        pltpu.make_async_copy(ref, ref, sem).wait()

    def forward_b(q):
        wait_bytes(own_b.at[q, pl.ds(1, OWNERS - 1)], gather_recv.at[q])
        send_z([
            (q, way, make(own_b.at[q], landing.at[q], zb_send.at[way, q], zb_recv.at[way, q], (t, to)))
            for way, _, landing, to in ways
        ], zb)

    def part_b(q):
        wait_z(q, zb)
        for n, both in enumerate(multiply(own_b[q], near_b[q], far_b[q], 1)):
            if q == 0:
                total_b[:, tile(n)] = both[0]
            elif q < QUADS - 1:
                total_b[:, tile(n)] += both[0]
            else:
                total = total_b[:, tile(n)] + both[0]
                out_ref[0, BINS:, tile(n)] = total[:BINS]
                out_ref[1, BINS:, tile(n)] = total[BINS:]

    def add_sums(k):
        lowest = 1 if k == 0 else 0
        wait_bytes(recv_sum.at[k, pl.ds(lowest, SIDE - lowest)], sum_recv.at[k])
        total = own_sum[...]
        for i in range(lowest, SIDE):
            total = total + recv_sum[k, i].astype(jnp.float32)
        if k < SIDE - 1:
            own_sum[...] = total
        else:
            out_ref[0, :BINS] = total[:BINS]
            out_ref[1, :BINS] = total[BINS:]

    for k in range(SIDE):
        forward_b(k)
        part_a(k)
    part_b(0)
    part_b(1)
    add_sums(0)
    add_sums(1)
    part_b(2)
    add_sums(2)
    part_b(3)
    add_sums(3)
    for q in range(QUADS):
        wait_bytes(stage_b.at[q, pl.ds(1, OWNERS - 1)], gather_send.at[q])
    for k in range(SIDE):
        lowest = 1 if k == 0 else 0
        wait_bytes(send_sum.at[k, pl.ds(lowest, SIDE - lowest)], sum_send.at[k])


def body(records, pair_list, live_count):
    tables = [jnp.asarray(table) for table in basis_tables()]
    any_space = pl.BlockSpec(memory_space=pl.ANY)
    vmem, bf16, f32 = pltpu.VMEM, jnp.bfloat16, jnp.float32
    dma = pltpu.SemaphoreType.DMA
    block_a = vmem((SIDE, SIDE, SEG, ROWS, CH), bf16)
    block_b = vmem((QUADS, OWNERS, 2, ROWS, CH), bf16)
    return pl.pallas_call(
        kernel,
        out_shape=vmem((2, 2 * BINS, PAIRS), f32),
        in_specs=[any_space] * 5,
        out_specs=pl.BlockSpec(memory_space=vmem),
        scratch_shapes=[
            vmem((2, SIDE, SIDE, ROWS, SAMPLES), bf16),
            vmem((SEG, SAMPLES, CH), bf16),
            vmem((2, PAIRS), jnp.int32),
            pltpu.SMEM((1,), jnp.int32),
            vmem((TILES, CH, TILE), bf16),
            vmem((TILES, 3 * CH, TILE), bf16),
            block_a,
            block_a,
            block_a,
            block_b,
            block_b,
            block_b,
            block_b,
            vmem((ROWS, PAIRS), f32),
            vmem((SIDE, SIDE, ROWS, PAIRS), bf16),
            vmem((SIDE, SIDE, ROWS, PAIRS), bf16),
            vmem((ROWS, PAIRS), f32),
            dma((4 + QUADS,)),
            dma((2, QUADS * EARLY + SIDE - EARLY)),
            dma((2, QUADS * EARLY + SIDE - EARLY)),
            dma((2, QUADS)),
            dma((2, QUADS)),
            dma((QUADS,)),
            dma((QUADS,)),
            dma((SIDE,)),
            dma((SIDE,)),
        ],
        compiler_params=pltpu.CompilerParams(
            collective_id=0, has_side_effects=True, vmem_limit_bytes=56 * 2**20
        ),
        cost_estimate=pl.CostEstimate(
            flops=7 * 10**9, bytes_accessed=4 * 2**20, transcendentals=0
        ),
    )(*tables, records, pair_list, live_count)


def solution(mesh):
    in_specs = (P("tm", None, "chan"), P(None, "chan"), P("chan"))
    out_specs = P(None, "tm", "chan")
    return jax.shard_map(body, mesh=mesh, in_specs=in_specs, out_specs=out_specs, check_vma=False)
```

```python
import functools
import math

import jax
import jax.numpy as jnp
import ml_dtypes
import numpy as np
from jax import lax
from jax.experimental import pallas as pl
from jax.experimental.pallas import tpu as pltpu
from jax.sharding import PartitionSpec as P

SAMPLES = 1024
NF = 256
BAND_LO = 16
EPSILON = 1e-06

SIDE = 4
SEG = 8
CH = 128
PAIRS = 1024
BINS = 16
ROWS = 2 * BINS
TILE = 256
TILES = PAIRS // TILE
QUADS = SEG // 2
MESH = pl.DeviceIdType.MESH

A_WAY = ((2, 2), (1, 2), (3, 2), (2, 1), (2, 3), (1, 1))
B_WAY = tuple((dy, dx) for dy in range(SIDE) for dx in range(SIDE) if (dy, dx) not in A_WAY)
GROUP = 2
PARTS = len(A_WAY) // GROUP
EARLY = 2


def basis_table():
    sample_ids = np.arange(SAMPLES, dtype=np.int64)
    bin_ids = np.arange(NF, dtype=np.int64) + BAND_LO
    phases = bin_ids[:, None] * sample_ids[None, :] % SAMPLES
    step = np.float32(2.0 * math.pi / SAMPLES)
    angles = phases.astype(np.float32) * step
    tapers = np.float32(0.5) - np.float32(0.5) * np.cos(sample_ids.astype(np.float32) * step)
    table = np.stack([np.cos(angles) * tapers[None, :], -np.sin(angles) * tapers[None, :]])
    table = table.astype(np.float32).astype(ml_dtypes.bfloat16)
    table = table.reshape(2, SIDE, SIDE, BINS, SAMPLES).transpose(1, 2, 0, 3, 4)
    ids = np.arange(2 * SIDE - 1) % SIDE
    return table.reshape(SIDE, SIDE, ROWS, SAMPLES)[ids[:, None], ids[None, :]]


def kernel(
    basis_hbm, rec_hbm, pair_hbm, live_hbm, out_ref,
    basis, rec, pair, live, w_left, w_right,
    own_a, near_a, far_a, stage_b, own_b, near_b, far_b, left_part, right_part, send_sum, recv_sum, total,
    in_sem, za_send, za_recv, zb_send, zb_recv, gather_send, gather_recv, sum_send, sum_recv,
):
    t = lax.axis_index("tm")
    c = lax.axis_index("chan")
    n_chan = lax.axis_size("chan")
    y, x = lax.div(t, SIDE), lax.rem(t, SIDE)
    side = 1 - 2 * lax.rem(c, 2)
    c_near, c_far = c + side, c - side
    has_far = jnp.logical_and(c_far >= 0, c_far < n_chan)
    one_far = jnp.where(has_far, 1, 0)
    ways = ((0, near_a, near_b, c_near), (1, far_a, far_b, c_far))

    def on_way(way, act):
        if way == 0:
            act()
        else:
            pl.when(has_far)(act)

    def peer(dy, dx):
        return (lax.rem(y + dy, SIDE) * SIDE + lax.rem(x + dx, SIDE), c)

    others = [to for to in A_WAY + B_WAY if to != (0, 0)]

    basis_copy = pltpu.make_async_copy(
        basis_hbm.at[pl.ds(y, SIDE), pl.ds(x, SIDE)], basis, in_sem.at[2]
    )
    rec_copies = [
        pltpu.make_async_copy(rec_hbm.at[pl.ds(2 * q, 2)], rec.at[pl.ds(2 * q, 2)], in_sem.at[3 + q])
        for q in range(QUADS)
    ]
    pair_copy = pltpu.make_async_copy(pair_hbm, pair, in_sem.at[0])
    live_copy = pltpu.make_async_copy(live_hbm, live, in_sem.at[1])
    rec_copies[0].start()
    basis_copy.start()
    for q in range(1, QUADS):
        rec_copies[q].start()
    pair_copy.start()
    live_copy.start()

    barrier = pltpu.get_barrier_semaphore()
    for to in [(t, c_near)] + [peer(dy, dx) for dy, dx in others]:
        pl.semaphore_signal(barrier, inc=1, device_id=to, device_id_type=MESH)

    @pl.when(has_far)
    def _():
        pl.semaphore_signal(barrier, inc=1, device_id=(t, c_far), device_id_type=MESH)

    @pl.when(jnp.logical_not(has_far))
    def _():
        far_a[...] = jnp.zeros_like(far_a)
        far_b[...] = jnp.zeros_like(far_b)

    def make(source, landing, send_sem, recv_sem, to):
        return pltpu.make_async_remote_copy(
            src_ref=source,
            dst_ref=landing,
            send_sem=send_sem,
            recv_sem=recv_sem,
            device_id=to,
            device_id_type=MESH,
        )

    za, zb = [], []

    def send_z(copies, started=za):
        started.extend(copies)
        for way in (1, 0):
            @functools.partial(on_way, way)
            def _():
                for _, w, copy in copies:
                    if w == way:
                        copy.start()

    def wait_z(k, way, started=za):
        @functools.partial(on_way, way)
        def _():
            for part, w, copy in started:
                if part == k and w == way:
                    copy.wait()

    basis_copy.wait()
    for q in range(QUADS):
        rec_copies[q].wait()
        wide = jnp.concatenate([rec[2 * q], rec[2 * q + 1]], axis=1)
        spectrum = jnp.dot(
            basis[...].reshape(2 * NF, SAMPLES), wide, preferred_element_type=jnp.float32
        )
        powers = jnp.sum(spectrum * spectrum, axis=0, keepdims=True) / NF
        white = (spectrum * lax.rsqrt(powers + EPSILON)).astype(jnp.bfloat16)
        for e in range(2):
            mine = white[:, e * CH:(e + 1) * CH].reshape(SIDE, SIDE, ROWS, CH)
            for i, (dy, dx) in enumerate(A_WAY):
                own_a[i // GROUP, i % GROUP, 2 * q + e] = mine[dy, dx]
            for i, (dy, dx) in enumerate(B_WAY):
                (own_b if i == 0 else stage_b)[q, i, e] = mine[dy, dx]
        if q == 0:
            pl.semaphore_wait(barrier, 1 + one_far + len(others))
        for k in range(EARLY):
            piece = (k, pl.ds(0, GROUP), pl.ds(2 * q, 2))
            sem = k * QUADS + q
            send_z([
                (k, way, make(own_a.at[piece], landing.at[piece], za_send.at[way, sem], za_recv.at[way, sem], (t, to)))
                for way, landing, _, to in ways
            ])
        for i, to in enumerate(B_WAY):
            if i > 0:
                make(
                    stage_b.at[q, i], own_b.at[q, i], gather_send.at[q], gather_recv.at[q], peer(*to)
                ).start()
    for k in range(EARLY, PARTS):
        sem = QUADS * EARLY + k - EARLY
        send_z([
            (k, way, make(own_a.at[k], landing.at[k], za_send.at[way, sem], za_recv.at[way, sem], (t, to)))
            for way, landing, _, to in ways
        ])

    pair_copy.wait()
    live_copy.wait()
    n_live = live[0]
    for n in range(TILES):
        cols = pl.ds(n * TILE, TILE)
        left = pair[0:1, cols] - c * CH
        right = pair[1:2, cols] - (c - 1) * CH
        slots = lax.broadcasted_iota(jnp.int32, (1, TILE), 1) + n * TILE
        left = jnp.where(slots < n_live, left, -1)
        ids = lax.broadcasted_iota(jnp.int32, (CH, TILE), 0)
        w_left[n] = jnp.where(ids == left, 1.0 / 128.0, 0.0).astype(jnp.bfloat16)
        for place, block in ((0, 1), (1, 1 + side), (2, 1 - side)):
            hot = jnp.where(ids + block * CH == right, 1.0, 0.0)
            w_right[n, pl.ds(place * CH, CH)] = hot.astype(jnp.bfloat16)

    def tile(n):
        return pl.ds(n * TILE, TILE)

    def before(own, near):
        mine = own.reshape(-1, CH)
        rows = pl.ds(0, mine.shape[0])
        wide = jnp.concatenate([mine, near.reshape(-1, CH)], axis=1)
        for n in range(TILES):
            left_part[n, rows] = jnp.dot(mine, w_left[n], preferred_element_type=jnp.float32)
            right_part[n, rows] = jnp.dot(
                wide, w_right[n, :2 * CH], preferred_element_type=jnp.float32
            )

    def after(far, groups):
        far = far.reshape(-1, CH)
        rows = pl.ds(0, far.shape[0])
        shape = (groups, far.shape[0] // (groups * ROWS), 2, BINS, TILE)
        sums = []
        for n in range(TILES):
            left = left_part[n, rows].reshape(shape)
            right = right_part[n, rows] + jnp.dot(
                far, w_right[n, 2 * CH:], preferred_element_type=jnp.float32
            )
            right = right.reshape(shape)
            real = jnp.sum(left[:, :, 0] * right[:, :, 0] + left[:, :, 1] * right[:, :, 1], axis=1)
            imag = jnp.sum(left[:, :, 1] * right[:, :, 0] - left[:, :, 0] * right[:, :, 1], axis=1)
            sums.append(jnp.concatenate([real, imag], axis=1))
        return sums

    def before_a(k):
        wait_z(k, 0)
        before(own_a[k], near_a[k])

    def after_a(k):
        wait_z(k, 1)
        for n, both in enumerate(after(far_a[k], GROUP)):
            send_sum[k, :, :, tile(n)] = both.astype(jnp.bfloat16)
        for i in range(GROUP):
            make(
                send_sum.at[k, i], recv_sum.at[k, i], sum_send.at[k], sum_recv.at[k],
                peer(*A_WAY[k * GROUP + i]),
            ).start()

    def wait_bytes(ref, sem):
        pltpu.make_async_copy(ref, ref, sem).wait()

    def forward_b(q):
        wait_bytes(own_b.at[q, pl.ds(1, len(B_WAY) - 1)], gather_recv.at[q])
        send_z([
            (q, way, make(own_b.at[q], landing.at[q], zb_send.at[way, q], zb_recv.at[way, q], (t, to)))
            for way, _, landing, to in ways
        ], zb)

    def before_b(q):
        wait_z(q, 0, zb)
        before(own_b[q], near_b[q])

    def after_b(q):
        wait_z(q, 1, zb)
        for n, both in enumerate(after(far_b[q], 1)):
            if q == 0:
                total[:, tile(n)] = both[0]
            elif q < QUADS - 1:
                total[:, tile(n)] += both[0]
            else:
                done = total[:, tile(n)] + both[0]
                out_ref[0, :, tile(n)] = done[:BINS]
                out_ref[1, :, tile(n)] = done[BINS:]

    def add_sums(k):
        wait_bytes(recv_sum.at[k], sum_recv.at[k])
        done = total[...]
        for i in range(GROUP):
            done = done + recv_sum[k, i].astype(jnp.float32)
        total[...] = done

    before_a(0)
    after_a(0)
    before_a(1)
    forward_b(0)
    after_a(1)
    forward_b(1)
    before_a(2)
    after_a(2)
    forward_b(2)
    before_b(0)
    forward_b(3)
    after_b(0)
    before_b(1)
    after_b(1)
    add_sums(0)
    before_b(2)
    after_b(2)
    before_b(3)
    add_sums(1)
    add_sums(2)
    after_b(3)
    for q in range(QUADS):
        wait_bytes(stage_b.at[q, pl.ds(1, len(B_WAY) - 1)], gather_send.at[q])
    for k in range(PARTS):
        wait_bytes(send_sum.at[k], sum_send.at[k])


def body(records, pair_list, live_count):
    table = jnp.asarray(basis_table())
    any_space = pl.BlockSpec(memory_space=pl.ANY)
    vmem, bf16, f32 = pltpu.VMEM, jnp.bfloat16, jnp.float32
    dma = pltpu.SemaphoreType.DMA
    block_a = vmem((PARTS, GROUP, SEG, ROWS, CH), bf16)
    block_b = vmem((QUADS, len(B_WAY), 2, ROWS, CH), bf16)
    parts = vmem((TILES, max(GROUP * SEG, 2 * len(B_WAY)) * ROWS, TILE), f32)
    sums = vmem((PARTS, GROUP, ROWS, PAIRS), bf16)
    return pl.pallas_call(
        kernel,
        out_shape=vmem((2, BINS, PAIRS), f32),
        in_specs=[any_space] * 4,
        out_specs=pl.BlockSpec(memory_space=vmem),
        scratch_shapes=[
            vmem((SIDE, SIDE, ROWS, SAMPLES), bf16),
            vmem((SEG, SAMPLES, CH), bf16),
            vmem((2, PAIRS), jnp.int32),
            pltpu.SMEM((1,), jnp.int32),
            vmem((TILES, CH, TILE), bf16),
            vmem((TILES, 3 * CH, TILE), bf16),
            block_a,
            block_a,
            block_a,
            block_b,
            block_b,
            block_b,
            block_b,
            parts,
            parts,
            sums,
            sums,
            vmem((ROWS, PAIRS), f32),
            dma((3 + QUADS,)),
            dma((2, QUADS * EARLY + PARTS - EARLY)),
            dma((2, QUADS * EARLY + PARTS - EARLY)),
            dma((2, QUADS)),
            dma((2, QUADS)),
            dma((QUADS,)),
            dma((QUADS,)),
            dma((PARTS,)),
            dma((PARTS,)),
        ],
        compiler_params=pltpu.CompilerParams(
            collective_id=0, has_side_effects=True, vmem_limit_bytes=56 * 2**20
        ),
        cost_estimate=pl.CostEstimate(
            flops=7 * 10**9, bytes_accessed=4 * 2**20, transcendentals=0
        ),
    )(table, records, pair_list, live_count)


def solution(mesh):
    in_specs = (P("tm", None, "chan"), P(None, "chan"), P("chan"))
    out_specs = P(None, "tm", "chan")
    return jax.shard_map(body, mesh=mesh, in_specs=in_specs, out_specs=out_specs, check_vma=False)
```

```python
import functools
import math

import jax
import jax.numpy as jnp
import ml_dtypes
import numpy as np
from jax import lax
from jax.experimental import pallas as pl
from jax.experimental.pallas import tpu as pltpu
from jax.sharding import PartitionSpec as P

SAMPLES = 1024
NF = 256
BAND_LO = 16
EPSILON = 1e-06

SIDE = 4
SEG = 8
CH = 128
PAIRS = 1024
BINS = 16
ROWS = 2 * BINS
TILE = 256
TILES = PAIRS // TILE
QUADS = SEG // 2
MESH = pl.DeviceIdType.MESH

A_WAY = ((2, 2), (1, 2), (3, 2), (2, 1), (2, 3), (0, 0))
B_WAY = tuple((dy, dx) for dy in range(SIDE) for dx in range(SIDE) if (dy, dx) not in A_WAY)
GROUP = 2
PARTS = len(A_WAY) // GROUP
SENT = tuple(GROUP - (k == PARTS - 1) for k in range(PARTS))
EARLY = 2


def basis_table():
    sample_ids = np.arange(SAMPLES, dtype=np.int64)
    bin_ids = np.arange(NF, dtype=np.int64) + BAND_LO
    phases = bin_ids[:, None] * sample_ids[None, :] % SAMPLES
    step = np.float32(2.0 * math.pi / SAMPLES)
    angles = phases.astype(np.float32) * step
    tapers = np.float32(0.5) - np.float32(0.5) * np.cos(sample_ids.astype(np.float32) * step)
    table = np.stack([np.cos(angles) * tapers[None, :], -np.sin(angles) * tapers[None, :]])
    table = table.astype(np.float32).astype(ml_dtypes.bfloat16)
    table = table.reshape(2, SIDE, SIDE, BINS, SAMPLES).transpose(1, 2, 0, 3, 4)
    ids = np.arange(2 * SIDE - 1) % SIDE
    return table.reshape(SIDE, SIDE, ROWS, SAMPLES)[ids[:, None], ids[None, :]]


def kernel(
    basis_hbm, rec_hbm, pair_hbm, live_hbm, out_ref,
    basis, rec, pair, live, w_left, w_right,
    own_a, near_a, far_a, stage_b, own_b, near_b, far_b, left_part, right_part, send_sum, recv_sum, total,
    in_sem, za_send, za_recv, zb_send, zb_recv, gather_send, gather_recv, sum_send, sum_recv,
):
    t = lax.axis_index("tm")
    c = lax.axis_index("chan")
    n_chan = lax.axis_size("chan")
    y, x = lax.div(t, SIDE), lax.rem(t, SIDE)
    side = 1 - 2 * lax.rem(c, 2)
    c_near, c_far = c + side, c - side
    has_far = jnp.logical_and(c_far >= 0, c_far < n_chan)
    one_far = jnp.where(has_far, 1, 0)
    ways = ((0, near_a, near_b, c_near), (1, far_a, far_b, c_far))

    def on_way(way, act):
        if way == 0:
            act()
        else:
            pl.when(has_far)(act)

    def peer(dy, dx):
        return (lax.rem(y + dy, SIDE) * SIDE + lax.rem(x + dx, SIDE), c)

    others = [to for to in A_WAY + B_WAY if to != (0, 0)]

    basis_copy = pltpu.make_async_copy(
        basis_hbm.at[pl.ds(y, SIDE), pl.ds(x, SIDE)], basis, in_sem.at[2]
    )
    rec_copies = [
        pltpu.make_async_copy(rec_hbm.at[pl.ds(2 * q, 2)], rec.at[pl.ds(2 * q, 2)], in_sem.at[3 + q])
        for q in range(QUADS)
    ]
    pair_copy = pltpu.make_async_copy(pair_hbm, pair, in_sem.at[0])
    live_copy = pltpu.make_async_copy(live_hbm, live, in_sem.at[1])
    rec_copies[0].start()
    basis_copy.start()
    for q in range(1, QUADS):
        rec_copies[q].start()
    pair_copy.start()
    live_copy.start()

    barrier = pltpu.get_barrier_semaphore()
    for to in [(t, c_near)] + [peer(dy, dx) for dy, dx in others]:
        pl.semaphore_signal(barrier, inc=1, device_id=to, device_id_type=MESH)

    @pl.when(has_far)
    def _():
        pl.semaphore_signal(barrier, inc=1, device_id=(t, c_far), device_id_type=MESH)

    @pl.when(jnp.logical_not(has_far))
    def _():
        far_a[...] = jnp.zeros_like(far_a)
        far_b[...] = jnp.zeros_like(far_b)

    def make(source, landing, send_sem, recv_sem, to):
        return pltpu.make_async_remote_copy(
            src_ref=source,
            dst_ref=landing,
            send_sem=send_sem,
            recv_sem=recv_sem,
            device_id=to,
            device_id_type=MESH,
        )

    za, zb = [], []

    def send_z(copies, started=za):
        started.extend(copies)
        for way in (1, 0):
            @functools.partial(on_way, way)
            def _():
                for _, w, copy in copies:
                    if w == way:
                        copy.start()

    def wait_z(k, way, started=za):
        @functools.partial(on_way, way)
        def _():
            for part, w, copy in started:
                if part == k and w == way:
                    copy.wait()

    basis_copy.wait()
    for q in range(QUADS):
        rec_copies[q].wait()
        wide = jnp.concatenate([rec[2 * q], rec[2 * q + 1]], axis=1)
        spectrum = jnp.dot(
            basis[...].reshape(2 * NF, SAMPLES), wide, preferred_element_type=jnp.float32
        )
        powers = jnp.sum(spectrum * spectrum, axis=0, keepdims=True) / NF
        white = (spectrum * lax.rsqrt(powers + EPSILON)).astype(jnp.bfloat16)
        for e in range(2):
            mine = white[:, e * CH:(e + 1) * CH].reshape(SIDE, SIDE, ROWS, CH)
            for i, (dy, dx) in enumerate(A_WAY):
                own_a[i // GROUP, i % GROUP, 2 * q + e] = mine[dy, dx]
            for i, (dy, dx) in enumerate(B_WAY):
                stage_b[q, i, e] = mine[dy, dx]
        if q == 0:
            pl.semaphore_wait(barrier, 1 + one_far + len(others))
        for k in range(EARLY):
            piece = (k, pl.ds(0, GROUP), pl.ds(2 * q, 2))
            sem = k * QUADS + q
            send_z([
                (k, way, make(own_a.at[piece], landing.at[piece], za_send.at[way, sem], za_recv.at[way, sem], (t, to)))
                for way, landing, _, to in ways
            ])
        for i, to in enumerate(B_WAY):
            make(
                stage_b.at[q, i], own_b.at[q, i], gather_send.at[q], gather_recv.at[q], peer(*to)
            ).start()
    for k in range(EARLY, PARTS):
        sem = QUADS * EARLY + k - EARLY
        send_z([
            (k, way, make(own_a.at[k], landing.at[k], za_send.at[way, sem], za_recv.at[way, sem], (t, to)))
            for way, landing, _, to in ways
        ])

    pair_copy.wait()
    live_copy.wait()
    n_live = live[0]
    for n in range(TILES):
        cols = pl.ds(n * TILE, TILE)
        left = pair[0:1, cols] - c * CH
        right = pair[1:2, cols] - (c - 1) * CH
        slots = lax.broadcasted_iota(jnp.int32, (1, TILE), 1) + n * TILE
        left = jnp.where(slots < n_live, left, -1)
        ids = lax.broadcasted_iota(jnp.int32, (CH, TILE), 0)
        w_left[n] = jnp.where(ids == left, 1.0 / 128.0, 0.0).astype(jnp.bfloat16)
        for place, block in ((0, 1), (1, 1 + side), (2, 1 - side)):
            hot = jnp.where(ids + block * CH == right, 1.0, 0.0)
            w_right[n, pl.ds(place * CH, CH)] = hot.astype(jnp.bfloat16)

    def tile(n):
        return pl.ds(n * TILE, TILE)

    def before(own, near):
        mine = own.reshape(-1, CH)
        rows = pl.ds(0, mine.shape[0])
        wide = jnp.concatenate([mine, near.reshape(-1, CH)], axis=1)
        for n in range(TILES):
            left_part[n, rows] = jnp.dot(mine, w_left[n], preferred_element_type=jnp.float32)
            right_part[n, rows] = jnp.dot(
                wide, w_right[n, :2 * CH], preferred_element_type=jnp.float32
            )

    def after(far, groups):
        far = far.reshape(-1, CH)
        rows = pl.ds(0, far.shape[0])
        shape = (groups, far.shape[0] // (groups * ROWS), 2, BINS, TILE)
        sums = []
        for n in range(TILES):
            left = left_part[n, rows].reshape(shape)
            right = right_part[n, rows] + jnp.dot(
                far, w_right[n, 2 * CH:], preferred_element_type=jnp.float32
            )
            right = right.reshape(shape)
            real = jnp.sum(left[:, :, 0] * right[:, :, 0] + left[:, :, 1] * right[:, :, 1], axis=1)
            imag = jnp.sum(left[:, :, 1] * right[:, :, 0] - left[:, :, 0] * right[:, :, 1], axis=1)
            sums.append(jnp.concatenate([real, imag], axis=1))
        return sums

    def before_a(k):
        wait_z(k, 0)
        before(own_a[k], near_a[k])

    def after_a(k):
        wait_z(k, 1)
        for n, both in enumerate(after(far_a[k], GROUP)):
            send_sum[k, :SENT[k], :, tile(n)] = both[:SENT[k]].astype(jnp.bfloat16)
            if SENT[k] < GROUP:
                total[:, tile(n)] = both[SENT[k]]
        for i in range(SENT[k]):
            make(
                send_sum.at[k, i], recv_sum.at[k, i], sum_send.at[k], sum_recv.at[k],
                peer(*A_WAY[k * GROUP + i]),
            ).start()

    def wait_bytes(ref, sem):
        pltpu.make_async_copy(ref, ref, sem).wait()

    def forward_b(q):
        wait_bytes(own_b.at[q], gather_recv.at[q])
        send_z([
            (q, way, make(own_b.at[q], landing.at[q], zb_send.at[way, q], zb_recv.at[way, q], (t, to)))
            for way, _, landing, to in ways
        ], zb)

    def before_b(q):
        wait_z(q, 0, zb)
        before(own_b[q], near_b[q])

    def after_b(q):
        wait_z(q, 1, zb)
        for n, both in enumerate(after(far_b[q], 1)):
            if q < QUADS - 1:
                total[:, tile(n)] += both[0]
            else:
                done = total[:, tile(n)] + both[0]
                out_ref[0, :, tile(n)] = done[:BINS]
                out_ref[1, :, tile(n)] = done[BINS:]

    def add_sums(k):
        wait_bytes(recv_sum.at[k, pl.ds(0, SENT[k])], sum_recv.at[k])
        done = total[...]
        for i in range(SENT[k]):
            done = done + recv_sum[k, i].astype(jnp.float32)
        total[...] = done

    for k in range(PARTS):
        forward_b(k)
        before_a(k)
        after_a(k)
    forward_b(3)
    before_b(0)
    after_b(0)
    before_b(1)
    after_b(1)
    add_sums(0)
    before_b(2)
    after_b(2)
    add_sums(1)
    before_b(3)
    add_sums(2)
    after_b(3)
    for q in range(QUADS):
        wait_bytes(stage_b.at[q], gather_send.at[q])
    for k in range(PARTS):
        wait_bytes(send_sum.at[k, pl.ds(0, SENT[k])], sum_send.at[k])


def body(records, pair_list, live_count):
    table = jnp.asarray(basis_table())
    any_space = pl.BlockSpec(memory_space=pl.ANY)
    vmem, bf16, f32 = pltpu.VMEM, jnp.bfloat16, jnp.float32
    dma = pltpu.SemaphoreType.DMA
    block_a = vmem((PARTS, GROUP, SEG, ROWS, CH), bf16)
    block_b = vmem((QUADS, len(B_WAY), 2, ROWS, CH), bf16)
    parts = vmem((TILES, max(GROUP * SEG, 2 * len(B_WAY)) * ROWS, TILE), f32)
    sums = vmem((PARTS, GROUP, ROWS, PAIRS), bf16)
    return pl.pallas_call(
        kernel,
        out_shape=vmem((2, BINS, PAIRS), f32),
        in_specs=[any_space] * 4,
        out_specs=pl.BlockSpec(memory_space=vmem),
        scratch_shapes=[
            vmem((SIDE, SIDE, ROWS, SAMPLES), bf16),
            vmem((SEG, SAMPLES, CH), bf16),
            vmem((2, PAIRS), jnp.int32),
            pltpu.SMEM((1,), jnp.int32),
            vmem((TILES, CH, TILE), bf16),
            vmem((TILES, 3 * CH, TILE), bf16),
            block_a,
            block_a,
            block_a,
            block_b,
            block_b,
            block_b,
            block_b,
            parts,
            parts,
            sums,
            sums,
            vmem((ROWS, PAIRS), f32),
            dma((3 + QUADS,)),
            dma((2, QUADS * EARLY + PARTS - EARLY)),
            dma((2, QUADS * EARLY + PARTS - EARLY)),
            dma((2, QUADS)),
            dma((2, QUADS)),
            dma((QUADS,)),
            dma((QUADS,)),
            dma((PARTS,)),
            dma((PARTS,)),
        ],
        compiler_params=pltpu.CompilerParams(
            collective_id=0, has_side_effects=True, vmem_limit_bytes=56 * 2**20
        ),
        cost_estimate=pl.CostEstimate(
            flops=7 * 10**9, bytes_accessed=4 * 2**20, transcendentals=0
        ),
    )(table, records, pair_list, live_count)


def solution(mesh):
    in_specs = (P("tm", None, "chan"), P(None, "chan"), P("chan"))
    out_specs = P(None, "tm", "chan")
    return jax.shard_map(body, mesh=mesh, in_specs=in_specs, out_specs=out_specs, check_vma=False)
```

```python
import functools
import math

import jax
import jax.numpy as jnp
import ml_dtypes
import numpy as np
from jax import lax
from jax.experimental import pallas as pl
from jax.experimental.pallas import tpu as pltpu
from jax.sharding import PartitionSpec as P

SAMPLES = 1024
NF = 256
BAND_LO = 16
EPSILON = 1e-06

SIDE = 4
OWNERS = SIDE * SIDE
SEG = 8
CH = 128
PAIRS = 1024
BINS = 8
ROWS = 2 * BINS
TILE = 256
TILES = PAIRS // TILE
QUADS = SEG // 2
MESH = pl.DeviceIdType.MESH


def basis_tables():
    sample_ids = np.arange(SAMPLES, dtype=np.int64)
    bin_ids = np.arange(NF, dtype=np.int64) + BAND_LO
    phases = bin_ids[:, None] * sample_ids[None, :] % SAMPLES
    step = np.float32(2.0 * math.pi / SAMPLES)
    angles = phases.astype(np.float32) * step
    tapers = np.float32(0.5) - np.float32(0.5) * np.cos(sample_ids.astype(np.float32) * step)
    table = np.stack([np.cos(angles) * tapers[None, :], -np.sin(angles) * tapers[None, :]])
    table = table.astype(np.float32).astype(ml_dtypes.bfloat16)
    table = table.reshape(2, SIDE, SIDE, 2, BINS, SAMPLES).transpose(3, 1, 2, 0, 4, 5)
    table = table.reshape(2, SIDE, SIDE, ROWS, SAMPLES)
    ids = np.arange(2 * SIDE - 1) % SIDE
    first = table[0][ids[None, :], (ids[:, None] + ids[None, :]) % SIDE]
    second = table[1][ids[:, None], ids[None, :]]
    return first, second


def kernel(
    basis_a_hbm, basis_b_hbm, rec_hbm, pair_hbm, live_hbm, out_ref,
    basis, rec, pair, live, w_left, w_right,
    own_a, near_a, far_a, stage_b, own_b, near_b, far_b, left_part, right_part, own_sum, send_sum, recv_sum, total_b,
    in_sem, za_send, za_recv, zb_send, zb_recv, gather_send, gather_recv, sum_send, sum_recv,
):
    t = lax.axis_index("tm")
    c = lax.axis_index("chan")
    n_chan = lax.axis_size("chan")
    y, x = lax.div(t, SIDE), lax.rem(t, SIDE)
    side = 1 - 2 * lax.rem(c, 2)
    c_near, c_far = c + side, c - side
    has_far = jnp.logical_and(c_far >= 0, c_far < n_chan)
    one_far = jnp.where(has_far, 1, 0)
    ways = ((0, near_a, near_b, c_near), (1, far_a, far_b, c_far))

    def on_way(way, act):
        if way == 0:
            act()
        else:
            pl.when(has_far)(act)

    def peer(dy, dx):
        return (lax.rem(y + dy, SIDE) * SIDE + lax.rem(x + dx, SIDE), c)

    others = [(dy, dx) for dy in (2, 1, 3, 0) for dx in (2, 1, 3, 0) if (dy, dx) != (0, 0)]

    skew = lax.rem(x - y + SIDE, SIDE)
    basis_copies = [
        pltpu.make_async_copy(table.at[pl.ds(u, SIDE), pl.ds(v, SIDE)], basis.at[h], in_sem.at[2 + h])
        for h, (table, u, v) in enumerate(((basis_a_hbm, skew, y), (basis_b_hbm, y, x)))
    ]
    rec_copies = [
        pltpu.make_async_copy(rec_hbm.at[pl.ds(2 * q, 2)], rec.at[pl.ds(2 * q, 2)], in_sem.at[4 + q])
        for q in range(QUADS)
    ]
    pair_copy = pltpu.make_async_copy(pair_hbm, pair, in_sem.at[0])
    live_copy = pltpu.make_async_copy(live_hbm, live, in_sem.at[1])
    rec_copies[0].start()
    for copy in basis_copies:
        copy.start()
    for q in range(1, QUADS):
        rec_copies[q].start()
    pair_copy.start()
    live_copy.start()

    barrier = pltpu.get_barrier_semaphore()
    for to in [(t, c_near)] + [peer(dy, dx) for dy, dx in others]:
        pl.semaphore_signal(barrier, inc=1, device_id=to, device_id_type=MESH)

    @pl.when(has_far)
    def _():
        pl.semaphore_signal(barrier, inc=1, device_id=(t, c_far), device_id_type=MESH)

    @pl.when(jnp.logical_not(has_far))
    def _():
        far_a[...] = jnp.zeros_like(far_a)
        far_b[...] = jnp.zeros_like(far_b)

    def make(source, landing, send_sem, recv_sem, to):
        return pltpu.make_async_remote_copy(
            src_ref=source,
            dst_ref=landing,
            send_sem=send_sem,
            recv_sem=recv_sem,
            device_id=to,
            device_id_type=MESH,
        )

    za, zb = [], []

    def send_z(copies, started=za):
        started.extend(copies)
        for way in (1, 0):
            @functools.partial(on_way, way)
            def _():
                for _, w, copy in copies:
                    if w == way:
                        copy.start()

    def wait_z(k, way, started=za):
        @functools.partial(on_way, way)
        def _():
            for part, w, copy in started:
                if part == k and w == way:
                    copy.wait()

    for copy in basis_copies:
        copy.wait()
    for q in range(QUADS):
        rec_copies[q].wait()
        wide = jnp.concatenate([rec[2 * q], rec[2 * q + 1]], axis=1)
        spectrum = jnp.dot(
            basis[...].reshape(2 * NF, SAMPLES), wide, preferred_element_type=jnp.float32
        )
        powers = jnp.sum(spectrum * spectrum, axis=0, keepdims=True) / NF
        white = (spectrum * lax.rsqrt(powers + EPSILON)).astype(jnp.bfloat16)
        for e in range(2):
            mine = white[:, e * CH:(e + 1) * CH].reshape(2, OWNERS, ROWS, CH)
            own_a[:, :, 2 * q + e] = mine[0].reshape(SIDE, SIDE, ROWS, CH)
            stage_b[q, :, e] = mine[1]
            own_b[q, 0, e] = mine[1, 0]
    pl.semaphore_wait(barrier, 1 + one_far + len(others))
    for q in range(QUADS):
        send_z([
            (q, way, make(own_a.at[q], landing.at[q], za_send.at[way, q], za_recv.at[way, q], (t, to)))
            for way, landing, _, to in ways
        ])
        for dy, dx in others:
            d = dy * SIDE + dx
            make(
                stage_b.at[q, d], own_b.at[q, d], gather_send.at[q], gather_recv.at[q], peer(dy, dx)
            ).start()

    pair_copy.wait()
    live_copy.wait()
    n_live = live[0]
    for n in range(TILES):
        cols = pl.ds(n * TILE, TILE)
        left = pair[0:1, cols] - c * CH
        right = pair[1:2, cols] - (c - 1) * CH
        slots = lax.broadcasted_iota(jnp.int32, (1, TILE), 1) + n * TILE
        left = jnp.where(slots < n_live, left, -1)
        ids = lax.broadcasted_iota(jnp.int32, (CH, TILE), 0)
        w_left[n] = jnp.where(ids == left, 1.0 / 128.0, 0.0).astype(jnp.bfloat16)
        for place, block in ((0, 1), (1, 1 + side), (2, 1 - side)):
            hot = jnp.where(ids + block * CH == right, 1.0, 0.0)
            w_right[n, pl.ds(place * CH, CH)] = hot.astype(jnp.bfloat16)

    def tile(n):
        return pl.ds(n * TILE, TILE)

    def before(own, near):
        mine = own.reshape(-1, CH)
        wide = jnp.concatenate([mine, near.reshape(-1, CH)], axis=1)
        for n in range(TILES):
            left_part[n] = jnp.dot(mine, w_left[n], preferred_element_type=jnp.float32)
            right_part[n] = jnp.dot(wide, w_right[n, :2 * CH], preferred_element_type=jnp.float32)

    def after(far, groups):
        far = far.reshape(-1, CH)
        shape = (groups, far.shape[0] // (groups * ROWS), 2, BINS, TILE)
        sums = []
        for n in range(TILES):
            left = left_part[n].reshape(shape)
            right = right_part[n] + jnp.dot(
                far, w_right[n, 2 * CH:], preferred_element_type=jnp.float32
            )
            right = right.reshape(shape)
            real = jnp.sum(left[:, :, 0] * right[:, :, 0] + left[:, :, 1] * right[:, :, 1], axis=1)
            imag = jnp.sum(left[:, :, 1] * right[:, :, 0] - left[:, :, 0] * right[:, :, 1], axis=1)
            sums.append(jnp.concatenate([real, imag], axis=1))
        return sums

    def before_a(k):
        wait_z(k, 0)
        before(own_a[k], near_a[k])

    def after_a(k):
        wait_z(k, 1)
        for n, both in enumerate(after(far_a[k], SIDE)):
            if k == 0:
                own_sum[:, tile(n)] = both[0]
            send_sum[k, :, :, tile(n)] = both.astype(jnp.bfloat16)
        for i in range(SIDE):
            dx = (i + k) % SIDE
            if (i, dx) != (0, 0):
                make(
                    send_sum.at[k, i], recv_sum.at[k, i], sum_send.at[k], sum_recv.at[k], peer(i, dx)
                ).start()

    def wait_bytes(ref, sem):
        pltpu.make_async_copy(ref, ref, sem).wait()

    def forward_b(q):
        wait_bytes(own_b.at[q, pl.ds(1, OWNERS - 1)], gather_recv.at[q])
        send_z([
            (q, way, make(own_b.at[q], landing.at[q], zb_send.at[way, q], zb_recv.at[way, q], (t, to)))
            for way, _, landing, to in ways
        ], zb)

    def before_b(q):
        wait_z(q, 0, zb)
        before(own_b[q], near_b[q])

    def after_b(q):
        wait_z(q, 1, zb)
        for n, both in enumerate(after(far_b[q], 1)):
            if q == 0:
                total_b[:, tile(n)] = both[0]
            elif q < QUADS - 1:
                total_b[:, tile(n)] += both[0]
            else:
                total = total_b[:, tile(n)] + both[0]
                out_ref[0, BINS:, tile(n)] = total[:BINS]
                out_ref[1, BINS:, tile(n)] = total[BINS:]

    def add_sums(k):
        lowest = 1 if k == 0 else 0
        wait_bytes(recv_sum.at[k, pl.ds(lowest, SIDE - lowest)], sum_recv.at[k])
        total = own_sum[...]
        for i in range(lowest, SIDE):
            total = total + recv_sum[k, i].astype(jnp.float32)
        if k < SIDE - 1:
            own_sum[...] = total
        else:
            out_ref[0, :BINS] = total[:BINS]
            out_ref[1, :BINS] = total[BINS:]

    before_a(0)
    after_a(0)
    before_a(1)
    forward_b(0)
    after_a(1)
    before_a(2)
    forward_b(1)
    after_a(2)
    before_a(3)
    after_a(3)
    forward_b(2)
    before_b(0)
    forward_b(3)
    after_b(0)
    before_b(1)
    after_b(1)
    add_sums(0)
    before_b(2)
    after_b(2)
    add_sums(1)
    before_b(3)
    add_sums(2)
    after_b(3)
    add_sums(3)
    for q in range(QUADS):
        wait_bytes(stage_b.at[q, pl.ds(1, OWNERS - 1)], gather_send.at[q])
    for k in range(SIDE):
        lowest = 1 if k == 0 else 0
        wait_bytes(send_sum.at[k, pl.ds(lowest, SIDE - lowest)], sum_send.at[k])


def body(records, pair_list, live_count):
    tables = [jnp.asarray(table) for table in basis_tables()]
    any_space = pl.BlockSpec(memory_space=pl.ANY)
    vmem, bf16, f32 = pltpu.VMEM, jnp.bfloat16, jnp.float32
    dma = pltpu.SemaphoreType.DMA
    block_a = vmem((SIDE, SIDE, SEG, ROWS, CH), bf16)
    block_b = vmem((QUADS, OWNERS, 2, ROWS, CH), bf16)
    parts = vmem((TILES, SIDE * SEG * ROWS, TILE), f32)
    return pl.pallas_call(
        kernel,
        out_shape=vmem((2, 2 * BINS, PAIRS), f32),
        in_specs=[any_space] * 5,
        out_specs=pl.BlockSpec(memory_space=vmem),
        scratch_shapes=[
            vmem((2, SIDE, SIDE, ROWS, SAMPLES), bf16),
            vmem((SEG, SAMPLES, CH), bf16),
            vmem((2, PAIRS), jnp.int32),
            pltpu.SMEM((1,), jnp.int32),
            vmem((TILES, CH, TILE), bf16),
            vmem((TILES, 3 * CH, TILE), bf16),
            block_a,
            block_a,
            block_a,
            block_b,
            block_b,
            block_b,
            block_b,
            parts,
            parts,
            vmem((ROWS, PAIRS), f32),
            vmem((SIDE, SIDE, ROWS, PAIRS), bf16),
            vmem((SIDE, SIDE, ROWS, PAIRS), bf16),
            vmem((ROWS, PAIRS), f32),
            dma((4 + QUADS,)),
            dma((2, SIDE)),
            dma((2, SIDE)),
            dma((2, QUADS)),
            dma((2, QUADS)),
            dma((QUADS,)),
            dma((QUADS,)),
            dma((SIDE,)),
            dma((SIDE,)),
        ],
        compiler_params=pltpu.CompilerParams(
            collective_id=0, has_side_effects=True, vmem_limit_bytes=56 * 2**20
        ),
        cost_estimate=pl.CostEstimate(
            flops=7 * 10**9, bytes_accessed=4 * 2**20, transcendentals=0
        ),
    )(*tables, records, pair_list, live_count)


def solution(mesh):
    in_specs = (P("tm", None, "chan"), P(None, "chan"), P("chan"))
    out_specs = P(None, "tm", "chan")
    return jax.shard_map(body, mesh=mesh, in_specs=in_specs, out_specs=out_specs, check_vma=False)
```

```python
import functools
import math

import jax
import jax.numpy as jnp
import ml_dtypes
import numpy as np
from jax import lax
from jax.experimental import pallas as pl
from jax.experimental.pallas import tpu as pltpu
from jax.sharding import PartitionSpec as P

SAMPLES = 1024
NF = 256
BAND_LO = 16
EPSILON = 1e-06

SIDE = 4
OWNERS = SIDE * SIDE
SEG = 8
CH = 128
PAIRS = 1024
BINS = 8
ROWS = 2 * BINS
TILE = 256
TILES = PAIRS // TILE
QUADS = SEG // 2
MESH = pl.DeviceIdType.MESH


PARTS = (
    ((2, 2), (1, 2), (3, 2), (2, 1)),
    ((2, 3), (1, 1), (1, 3), (3, 1)),
    ((3, 3), (0, 2), (2, 0), (0, 1)),
    ((0, 3), (1, 0), (3, 0), (0, 0)),
)
SENT = tuple(sum(to != (0, 0) for to in part) for part in PARTS)
EARLY = 2


def basis_table():
    sample_ids = np.arange(SAMPLES, dtype=np.int64)
    bin_ids = np.arange(NF, dtype=np.int64) + BAND_LO
    phases = bin_ids[:, None] * sample_ids[None, :] % SAMPLES
    step = np.float32(2.0 * math.pi / SAMPLES)
    angles = phases.astype(np.float32) * step
    tapers = np.float32(0.5) - np.float32(0.5) * np.cos(sample_ids.astype(np.float32) * step)
    table = np.stack([np.cos(angles) * tapers[None, :], -np.sin(angles) * tapers[None, :]])
    table = table.astype(np.float32).astype(ml_dtypes.bfloat16)
    table = table.reshape(2, SIDE, SIDE, 2, BINS, SAMPLES).transpose(1, 2, 3, 0, 4, 5)
    ids = np.arange(2 * SIDE - 1) % SIDE
    return table.reshape(SIDE, SIDE, 2, ROWS, SAMPLES)[ids[:, None], ids[None, :]]


def kernel(
    basis_hbm, rec_hbm, pair_hbm, live_hbm, out_ref,
    basis, rec, pair, live, w_left, w_right,
    own_a, near_a, far_a, stage_b, own_b, near_b, far_b, left_part, right_part, own_sum, send_sum, recv_sum, total_b,
    in_sem, za_send, za_recv, zb_send, zb_recv, gather_send, gather_recv, sum_send, sum_recv,
):
    t = lax.axis_index("tm")
    c = lax.axis_index("chan")
    n_chan = lax.axis_size("chan")
    y, x = lax.div(t, SIDE), lax.rem(t, SIDE)
    side = 1 - 2 * lax.rem(c, 2)
    c_near, c_far = c + side, c - side
    has_far = jnp.logical_and(c_far >= 0, c_far < n_chan)
    one_far = jnp.where(has_far, 1, 0)
    ways = ((0, near_a, near_b, c_near), (1, far_a, far_b, c_far))

    def on_way(way, act):
        if way == 0:
            act()
        else:
            pl.when(has_far)(act)

    def peer(dy, dx):
        return (lax.rem(y + dy, SIDE) * SIDE + lax.rem(x + dx, SIDE), c)

    others = [to for part in PARTS for to in part if to != (0, 0)]

    basis_copy = pltpu.make_async_copy(
        basis_hbm.at[pl.ds(y, SIDE), pl.ds(x, SIDE)], basis, in_sem.at[2]
    )
    rec_copies = [
        pltpu.make_async_copy(rec_hbm.at[pl.ds(2 * q, 2)], rec.at[pl.ds(2 * q, 2)], in_sem.at[3 + q])
        for q in range(QUADS)
    ]
    pair_copy = pltpu.make_async_copy(pair_hbm, pair, in_sem.at[0])
    live_copy = pltpu.make_async_copy(live_hbm, live, in_sem.at[1])
    rec_copies[0].start()
    basis_copy.start()

    barrier = pltpu.get_barrier_semaphore()
    for to in [(t, c_near)] + [peer(dy, dx) for dy, dx in others]:
        pl.semaphore_signal(barrier, inc=1, device_id=to, device_id_type=MESH)

    @pl.when(has_far)
    def _():
        pl.semaphore_signal(barrier, inc=1, device_id=(t, c_far), device_id_type=MESH)

    for q in range(1, QUADS):
        rec_copies[q].start()
    pair_copy.start()
    live_copy.start()

    @pl.when(jnp.logical_not(has_far))
    def _():
        far_a[...] = jnp.zeros_like(far_a)
        far_b[...] = jnp.zeros_like(far_b)

    def make(source, landing, send_sem, recv_sem, to):
        return pltpu.make_async_remote_copy(
            src_ref=source,
            dst_ref=landing,
            send_sem=send_sem,
            recv_sem=recv_sem,
            device_id=to,
            device_id_type=MESH,
        )

    za, zb = [], []

    def send_z(copies, started=za):
        started.extend(copies)
        for way in (1, 0):
            @functools.partial(on_way, way)
            def _():
                for _, w, copy in copies:
                    if w == way:
                        copy.start()

    def wait_z(k, way, started=za):
        @functools.partial(on_way, way)
        def _():
            for part, w, copy in started:
                if part == k and w == way:
                    copy.wait()

    basis_copy.wait()
    for q in range(QUADS):
        rec_copies[q].wait()
        wide = jnp.concatenate([rec[2 * q], rec[2 * q + 1]], axis=1)
        spectrum = jnp.dot(
            basis[...].reshape(2 * NF, SAMPLES), wide, preferred_element_type=jnp.float32
        )
        powers = jnp.sum(spectrum * spectrum, axis=0, keepdims=True) / NF
        white = (spectrum * lax.rsqrt(powers + EPSILON)).astype(jnp.bfloat16)
        for e in range(2):
            mine = white[:, e * CH:(e + 1) * CH].reshape(SIDE, SIDE, 2, ROWS, CH)
            for k, part in enumerate(PARTS):
                for i, (dy, dx) in enumerate(part):
                    own_a[k, i, 2 * q + e] = mine[dy, dx, 0]
            stage_b[q, :, e] = mine[:, :, 1].reshape(OWNERS, ROWS, CH)
            own_b[q, 0, e] = mine[0, 0, 1]
        if q == 0:
            pl.semaphore_wait(barrier, 1 + one_far + len(others))
        for k in range(EARLY):
            piece = (k, pl.ds(0, SIDE), pl.ds(2 * q, 2))
            sem = k * QUADS + q
            send_z([
                (k, way, make(own_a.at[piece], landing.at[piece], za_send.at[way, sem], za_recv.at[way, sem], (t, to)))
                for way, landing, _, to in ways
            ])
        for dy, dx in others:
            d = dy * SIDE + dx
            make(
                stage_b.at[q, d], own_b.at[q, d], gather_send.at[q], gather_recv.at[q], peer(dy, dx)
            ).start()
    for k in range(EARLY, SIDE):
        sem = QUADS * EARLY + k - EARLY
        send_z([
            (k, way, make(own_a.at[k], landing.at[k], za_send.at[way, sem], za_recv.at[way, sem], (t, to)))
            for way, landing, _, to in ways
        ])

    pair_copy.wait()
    live_copy.wait()
    n_live = live[0]
    for n in range(TILES):
        cols = pl.ds(n * TILE, TILE)
        left = pair[0:1, cols] - c * CH
        right = pair[1:2, cols] - (c - 1) * CH
        slots = lax.broadcasted_iota(jnp.int32, (1, TILE), 1) + n * TILE
        left = jnp.where(slots < n_live, left, -1)
        ids = lax.broadcasted_iota(jnp.int32, (CH, TILE), 0)
        w_left[n] = jnp.where(ids == left, 1.0 / 128.0, 0.0).astype(jnp.bfloat16)
        for place, block in ((0, 1), (1, 1 + side), (2, 1 - side)):
            hot = jnp.where(ids + block * CH == right, 1.0, 0.0)
            w_right[n, pl.ds(place * CH, CH)] = hot.astype(jnp.bfloat16)

    def tile(n):
        return pl.ds(n * TILE, TILE)

    def before(own, near):
        mine = own.reshape(-1, CH)
        wide = jnp.concatenate([mine, near.reshape(-1, CH)], axis=1)
        for n in range(TILES):
            left_part[n] = jnp.dot(mine, w_left[n], preferred_element_type=jnp.float32)
            right_part[n] = jnp.dot(wide, w_right[n, :2 * CH], preferred_element_type=jnp.float32)

    def after(far, groups):
        far = far.reshape(-1, CH)
        shape = (groups, far.shape[0] // (groups * ROWS), 2, BINS, TILE)
        sums = []
        for n in range(TILES):
            left = left_part[n].reshape(shape)
            right = right_part[n] + jnp.dot(
                far, w_right[n, 2 * CH:], preferred_element_type=jnp.float32
            )
            right = right.reshape(shape)
            real = jnp.sum(left[:, :, 0] * right[:, :, 0] + left[:, :, 1] * right[:, :, 1], axis=1)
            imag = jnp.sum(left[:, :, 1] * right[:, :, 0] - left[:, :, 0] * right[:, :, 1], axis=1)
            sums.append(jnp.concatenate([real, imag], axis=1))
        return sums

    def before_a(k):
        wait_z(k, 0)
        before(own_a[k], near_a[k])

    def after_a(k):
        wait_z(k, 1)
        for n, both in enumerate(after(far_a[k], SIDE)):
            send_sum[k, :SENT[k], :, tile(n)] = both[:SENT[k]].astype(jnp.bfloat16)
            if SENT[k] < SIDE:
                own_sum[:, tile(n)] = both[SENT[k]]
        for i in range(SENT[k]):
            make(
                send_sum.at[k, i], recv_sum.at[k, i], sum_send.at[k], sum_recv.at[k], peer(*PARTS[k][i])
            ).start()

    def wait_bytes(ref, sem):
        pltpu.make_async_copy(ref, ref, sem).wait()

    def forward_b(q):
        wait_bytes(own_b.at[q, pl.ds(1, OWNERS - 1)], gather_recv.at[q])
        send_z([
            (q, way, make(own_b.at[q], landing.at[q], zb_send.at[way, q], zb_recv.at[way, q], (t, to)))
            for way, _, landing, to in ways
        ], zb)

    def before_b(q):
        wait_z(q, 0, zb)
        before(own_b[q], near_b[q])

    def after_b(q):
        wait_z(q, 1, zb)
        for n, both in enumerate(after(far_b[q], 1)):
            if q == 0:
                total_b[:, tile(n)] = both[0]
            elif q < QUADS - 1:
                total_b[:, tile(n)] += both[0]
            else:
                total = total_b[:, tile(n)] + both[0]
                out_ref[0, BINS:, tile(n)] = total[:BINS]
                out_ref[1, BINS:, tile(n)] = total[BINS:]

    def add_sums(k):
        wait_bytes(recv_sum.at[k, pl.ds(0, SENT[k])], sum_recv.at[k])
        total = own_sum[...]
        for i in range(SENT[k]):
            total = total + recv_sum[k, i].astype(jnp.float32)
        if k < SIDE - 1:
            own_sum[...] = total
        else:
            out_ref[0, :BINS] = total[:BINS]
            out_ref[1, :BINS] = total[BINS:]

    for k in range(SIDE):
        forward_b(k)
        before_a(k)
        after_a(k)
    before_b(0)
    after_b(0)
    before_b(1)
    after_b(1)
    add_sums(0)
    add_sums(1)
    before_b(2)
    after_b(2)
    add_sums(2)
    before_b(3)
    add_sums(3)
    after_b(3)
    for q in range(QUADS):
        wait_bytes(stage_b.at[q, pl.ds(1, OWNERS - 1)], gather_send.at[q])
    for k in range(SIDE):
        wait_bytes(send_sum.at[k, pl.ds(0, SENT[k])], sum_send.at[k])


def body(records, pair_list, live_count):
    table = jnp.asarray(basis_table())
    any_space = pl.BlockSpec(memory_space=pl.ANY)
    vmem, bf16, f32 = pltpu.VMEM, jnp.bfloat16, jnp.float32
    dma = pltpu.SemaphoreType.DMA
    block_a = vmem((SIDE, SIDE, SEG, ROWS, CH), bf16)
    block_b = vmem((QUADS, OWNERS, 2, ROWS, CH), bf16)
    parts = vmem((TILES, SIDE * SEG * ROWS, TILE), f32)
    return pl.pallas_call(
        kernel,
        out_shape=vmem((2, 2 * BINS, PAIRS), f32),
        in_specs=[any_space] * 4,
        out_specs=pl.BlockSpec(memory_space=vmem),
        scratch_shapes=[
            vmem((SIDE, SIDE, 2, ROWS, SAMPLES), bf16),
            vmem((SEG, SAMPLES, CH), bf16),
            vmem((2, PAIRS), jnp.int32),
            pltpu.SMEM((1,), jnp.int32),
            vmem((TILES, CH, TILE), bf16),
            vmem((TILES, 3 * CH, TILE), bf16),
            block_a,
            block_a,
            block_a,
            block_b,
            block_b,
            block_b,
            block_b,
            parts,
            parts,
            vmem((ROWS, PAIRS), f32),
            vmem((SIDE, SIDE, ROWS, PAIRS), bf16),
            vmem((SIDE, SIDE, ROWS, PAIRS), bf16),
            vmem((ROWS, PAIRS), f32),
            dma((3 + QUADS,)),
            dma((2, QUADS * EARLY + SIDE - EARLY)),
            dma((2, QUADS * EARLY + SIDE - EARLY)),
            dma((2, QUADS)),
            dma((2, QUADS)),
            dma((QUADS,)),
            dma((QUADS,)),
            dma((SIDE,)),
            dma((SIDE,)),
        ],
        compiler_params=pltpu.CompilerParams(
            collective_id=0, has_side_effects=True, vmem_limit_bytes=56 * 2**20
        ),
        cost_estimate=pl.CostEstimate(
            flops=7 * 10**9, bytes_accessed=4 * 2**20, transcendentals=0
        ),
    )(table, records, pair_list, live_count)


def solution(mesh):
    in_specs = (P("tm", None, "chan"), P(None, "chan"), P("chan"))
    out_specs = P(None, "tm", "chan")
    return jax.shard_map(body, mesh=mesh, in_specs=in_specs, out_specs=out_specs, check_vma=False)
```

```python
import functools
import math

import jax
import jax.numpy as jnp
import ml_dtypes
import numpy as np
from jax import lax
from jax.experimental import pallas as pl
from jax.experimental.pallas import tpu as pltpu
from jax.sharding import PartitionSpec as P

SAMPLES = 1024
NF = 256
BAND_LO = 16
EPSILON = 1e-06

SIDE = 4
OWNERS = SIDE * SIDE
SEG = 8
CH = 128
PAIRS = 1024
BINS = 8
ROWS = 2 * BINS
TILE = 256
TILES = PAIRS // TILE
QUADS = SEG // 2
EARLY = 2
MESH = pl.DeviceIdType.MESH


def basis_tables():
    sample_ids = np.arange(SAMPLES, dtype=np.int64)
    bin_ids = np.arange(NF, dtype=np.int64) + BAND_LO
    phases = bin_ids[:, None] * sample_ids[None, :] % SAMPLES
    step = np.float32(2.0 * math.pi / SAMPLES)
    angles = phases.astype(np.float32) * step
    tapers = np.float32(0.5) - np.float32(0.5) * np.cos(sample_ids.astype(np.float32) * step)
    table = np.stack([np.cos(angles) * tapers[None, :], -np.sin(angles) * tapers[None, :]])
    table = table.astype(np.float32).astype(ml_dtypes.bfloat16)
    table = table.reshape(2, SIDE, SIDE, 2, BINS, SAMPLES).transpose(3, 1, 2, 0, 4, 5)
    table = table.reshape(2, SIDE, SIDE, ROWS, SAMPLES)
    ids = np.arange(2 * SIDE - 1) % SIDE
    first = table[0][ids[None, :], (ids[:, None] + ids[None, :]) % SIDE]
    second = table[1][ids[:, None], ids[None, :]]
    return first, second


def kernel(
    basis_a_hbm, basis_b_hbm, rec_hbm, pair_hbm, live_hbm, out_ref,
    basis, rec, pair, live, w_left, w_right,
    own_a, near_a, far_a, stage_b, own_b, near_b, far_b, left_part, right_part, own_sum, send_sum, recv_sum, total_b,
    in_sem, za_send, za_recv, zb_send, zb_recv, gather_send, gather_recv, sum_send, sum_recv,
):
    t = lax.axis_index("tm")
    c = lax.axis_index("chan")
    n_chan = lax.axis_size("chan")
    y, x = lax.div(t, SIDE), lax.rem(t, SIDE)
    side = 1 - 2 * lax.rem(c, 2)
    c_near, c_far = c + side, c - side
    has_far = jnp.logical_and(c_far >= 0, c_far < n_chan)
    one_far = jnp.where(has_far, 1, 0)
    ways = ((0, near_a, near_b, c_near), (1, far_a, far_b, c_far))

    def on_way(way, act):
        if way == 0:
            act()
        else:
            pl.when(has_far)(act)

    def peer(dy, dx):
        return (lax.rem(y + dy, SIDE) * SIDE + lax.rem(x + dx, SIDE), c)

    others = [(dy, dx) for dy in (2, 1, 3, 0) for dx in (2, 1, 3, 0) if (dy, dx) != (0, 0)]

    skew = lax.rem(x - y + SIDE, SIDE)
    basis_copies = [
        pltpu.make_async_copy(table.at[pl.ds(u, SIDE), pl.ds(v, SIDE)], basis.at[h], in_sem.at[2 + h])
        for h, (table, u, v) in enumerate(((basis_a_hbm, skew, y), (basis_b_hbm, y, x)))
    ]
    rec_copies = [
        pltpu.make_async_copy(rec_hbm.at[pl.ds(2 * q, 2)], rec.at[pl.ds(2 * q, 2)], in_sem.at[4 + q])
        for q in range(QUADS)
    ]
    pair_copy = pltpu.make_async_copy(pair_hbm, pair, in_sem.at[0])
    live_copy = pltpu.make_async_copy(live_hbm, live, in_sem.at[1])
    rec_copies[0].start()
    for copy in basis_copies:
        copy.start()
    for q in range(1, QUADS):
        rec_copies[q].start()
    pair_copy.start()
    live_copy.start()

    barrier = pltpu.get_barrier_semaphore()
    for to in [(t, c_near)] + [peer(dy, dx) for dy, dx in others]:
        pl.semaphore_signal(barrier, inc=1, device_id=to, device_id_type=MESH)

    @pl.when(has_far)
    def _():
        pl.semaphore_signal(barrier, inc=1, device_id=(t, c_far), device_id_type=MESH)

    @pl.when(jnp.logical_not(has_far))
    def _():
        far_a[...] = jnp.zeros_like(far_a)
        far_b[...] = jnp.zeros_like(far_b)

    def make(source, landing, send_sem, recv_sem, to):
        return pltpu.make_async_remote_copy(
            src_ref=source,
            dst_ref=landing,
            send_sem=send_sem,
            recv_sem=recv_sem,
            device_id=to,
            device_id_type=MESH,
        )

    za, zb = [], []

    def send_z(copies, started=za):
        started.extend(copies)
        for way in (1, 0):
            @functools.partial(on_way, way)
            def _():
                for _, w, copy in copies:
                    if w == way:
                        copy.start()

    def wait_z(k, way, started=za):
        @functools.partial(on_way, way)
        def _():
            for part, w, copy in started:
                if part == k and w == way:
                    copy.wait()

    for copy in basis_copies:
        copy.wait()
    for q in range(QUADS):
        rec_copies[q].wait()
        wide = jnp.concatenate([rec[2 * q], rec[2 * q + 1]], axis=1)
        spectrum = jnp.dot(
            basis[...].reshape(2 * NF, SAMPLES), wide, preferred_element_type=jnp.float32
        )
        powers = jnp.sum(spectrum * spectrum, axis=0, keepdims=True) / NF
        white = (spectrum * lax.rsqrt(powers + EPSILON)).astype(jnp.bfloat16)
        for e in range(2):
            mine = white[:, e * CH:(e + 1) * CH].reshape(2, OWNERS, ROWS, CH)
            own_a[:, :, 2 * q + e] = mine[0].reshape(SIDE, SIDE, ROWS, CH)
            stage_b[q, :, e] = mine[1]
            own_b[q, 0, e] = mine[1, 0]
        if q == 0:
            pl.semaphore_wait(barrier, 1 + one_far + len(others))
        for k in range(EARLY):
            piece = (k, pl.ds(0, SIDE), pl.ds(2 * q, 2))
            sem = k * QUADS + q
            send_z([
                (k, way, make(own_a.at[piece], landing.at[piece], za_send.at[way, sem], za_recv.at[way, sem], (t, to)))
                for way, landing, _, to in ways
            ])
        for dy, dx in others:
            d = dy * SIDE + dx
            make(
                stage_b.at[q, d], own_b.at[q, d], gather_send.at[q], gather_recv.at[q], peer(dy, dx)
            ).start()
    for k in range(EARLY, SIDE):
        sem = QUADS * EARLY + k - EARLY
        send_z([
            (k, way, make(own_a.at[k], landing.at[k], za_send.at[way, sem], za_recv.at[way, sem], (t, to)))
            for way, landing, _, to in ways
        ])

    pair_copy.wait()
    live_copy.wait()
    n_live = live[0]
    for n in range(TILES):
        cols = pl.ds(n * TILE, TILE)
        left = pair[0:1, cols] - c * CH
        right = pair[1:2, cols] - (c - 1) * CH
        slots = lax.broadcasted_iota(jnp.int32, (1, TILE), 1) + n * TILE
        left = jnp.where(slots < n_live, left, -1)
        ids = lax.broadcasted_iota(jnp.int32, (CH, TILE), 0)
        w_left[n] = jnp.where(ids == left, 1.0 / 128.0, 0.0).astype(jnp.bfloat16)
        for place, block in ((0, 1), (1, 1 + side), (2, 1 - side)):
            hot = jnp.where(ids + block * CH == right, 1.0, 0.0)
            w_right[n, pl.ds(place * CH, CH)] = hot.astype(jnp.bfloat16)

    def tile(n):
        return pl.ds(n * TILE, TILE)

    def before(own, near):
        mine = own.reshape(-1, CH)
        wide = jnp.concatenate([mine, near.reshape(-1, CH)], axis=1)
        for n in range(TILES):
            left_part[n] = jnp.dot(mine, w_left[n], preferred_element_type=jnp.float32)
            right_part[n] = jnp.dot(wide, w_right[n, :2 * CH], preferred_element_type=jnp.float32)

    def after(far, groups):
        far = far.reshape(-1, CH)
        shape = (groups, far.shape[0] // (groups * ROWS), 2, BINS, TILE)
        sums = []
        for n in range(TILES):
            left = left_part[n].reshape(shape)
            right = right_part[n] + jnp.dot(
                far, w_right[n, 2 * CH:], preferred_element_type=jnp.float32
            )
            right = right.reshape(shape)
            real = jnp.sum(left[:, :, 0] * right[:, :, 0] + left[:, :, 1] * right[:, :, 1], axis=1)
            imag = jnp.sum(left[:, :, 1] * right[:, :, 0] - left[:, :, 0] * right[:, :, 1], axis=1)
            sums.append(jnp.concatenate([real, imag], axis=1))
        return sums

    def before_a(k):
        wait_z(k, 0)
        before(own_a[k], near_a[k])

    def after_a(k):
        wait_z(k, 1)
        for n, both in enumerate(after(far_a[k], SIDE)):
            if k == 0:
                own_sum[:, tile(n)] = both[0]
            send_sum[k, :, :, tile(n)] = both.astype(jnp.bfloat16)
        for i in range(SIDE):
            dx = (i + k) % SIDE
            if (i, dx) != (0, 0):
                make(
                    send_sum.at[k, i], recv_sum.at[k, i], sum_send.at[k], sum_recv.at[k], peer(i, dx)
                ).start()

    def wait_bytes(ref, sem):
        pltpu.make_async_copy(ref, ref, sem).wait()

    def forward_b(q):
        wait_bytes(own_b.at[q, pl.ds(1, OWNERS - 1)], gather_recv.at[q])
        send_z([
            (q, way, make(own_b.at[q], landing.at[q], zb_send.at[way, q], zb_recv.at[way, q], (t, to)))
            for way, _, landing, to in ways
        ], zb)

    def before_b(q):
        wait_z(q, 0, zb)
        before(own_b[q], near_b[q])

    def after_b(q):
        wait_z(q, 1, zb)
        for n, both in enumerate(after(far_b[q], 1)):
            if q == 0:
                total_b[:, tile(n)] = both[0]
            elif q < QUADS - 1:
                total_b[:, tile(n)] += both[0]
            else:
                total = total_b[:, tile(n)] + both[0]
                out_ref[0, BINS:, tile(n)] = total[:BINS]
                out_ref[1, BINS:, tile(n)] = total[BINS:]

    def add_sums(k):
        lowest = 1 if k == 0 else 0
        wait_bytes(recv_sum.at[k, pl.ds(lowest, SIDE - lowest)], sum_recv.at[k])
        total = own_sum[...]
        for i in range(lowest, SIDE):
            total = total + recv_sum[k, i].astype(jnp.float32)
        if k < SIDE - 1:
            own_sum[...] = total
        else:
            out_ref[0, :BINS] = total[:BINS]
            out_ref[1, :BINS] = total[BINS:]

    before_a(0)
    after_a(0)
    before_a(1)
    forward_b(0)
    after_a(1)
    before_a(2)
    forward_b(1)
    after_a(2)
    before_a(3)
    forward_b(2)
    after_a(3)
    before_b(0)
    forward_b(3)
    after_b(0)
    before_b(1)
    after_b(1)
    add_sums(0)
    before_b(2)
    after_b(2)
    add_sums(1)
    before_b(3)
    add_sums(2)
    after_b(3)
    add_sums(3)
    for q in range(QUADS):
        wait_bytes(stage_b.at[q, pl.ds(1, OWNERS - 1)], gather_send.at[q])
    for k in range(SIDE):
        lowest = 1 if k == 0 else 0
        wait_bytes(send_sum.at[k, pl.ds(lowest, SIDE - lowest)], sum_send.at[k])


def body(records, pair_list, live_count):
    tables = [jnp.asarray(table) for table in basis_tables()]
    any_space = pl.BlockSpec(memory_space=pl.ANY)
    vmem, bf16, f32 = pltpu.VMEM, jnp.bfloat16, jnp.float32
    dma = pltpu.SemaphoreType.DMA
    block_a = vmem((SIDE, SIDE, SEG, ROWS, CH), bf16)
    block_b = vmem((QUADS, OWNERS, 2, ROWS, CH), bf16)
    parts = vmem((TILES, SIDE * SEG * ROWS, TILE), f32)
    return pl.pallas_call(
        kernel,
        out_shape=vmem((2, 2 * BINS, PAIRS), f32),
        in_specs=[any_space] * 5,
        out_specs=pl.BlockSpec(memory_space=vmem),
        scratch_shapes=[
            vmem((2, SIDE, SIDE, ROWS, SAMPLES), bf16),
            vmem((SEG, SAMPLES, CH), bf16),
            vmem((2, PAIRS), jnp.int32),
            pltpu.SMEM((1,), jnp.int32),
            vmem((TILES, CH, TILE), bf16),
            vmem((TILES, 3 * CH, TILE), bf16),
            block_a,
            block_a,
            block_a,
            block_b,
            block_b,
            block_b,
            block_b,
            parts,
            parts,
            vmem((ROWS, PAIRS), f32),
            vmem((SIDE, SIDE, ROWS, PAIRS), bf16),
            vmem((SIDE, SIDE, ROWS, PAIRS), bf16),
            vmem((ROWS, PAIRS), f32),
            dma((4 + QUADS,)),
            dma((2, QUADS * EARLY + SIDE - EARLY)),
            dma((2, QUADS * EARLY + SIDE - EARLY)),
            dma((2, QUADS)),
            dma((2, QUADS)),
            dma((QUADS,)),
            dma((QUADS,)),
            dma((SIDE,)),
            dma((SIDE,)),
        ],
        compiler_params=pltpu.CompilerParams(
            collective_id=0, has_side_effects=True, vmem_limit_bytes=56 * 2**20
        ),
        cost_estimate=pl.CostEstimate(
            flops=7 * 10**9, bytes_accessed=4 * 2**20, transcendentals=0
        ),
    )(*tables, records, pair_list, live_count)


def solution(mesh):
    in_specs = (P("tm", None, "chan"), P(None, "chan"), P("chan"))
    out_specs = P(None, "tm", "chan")
    return jax.shard_map(body, mesh=mesh, in_specs=in_specs, out_specs=out_specs, check_vma=False)
```

```python
import functools
import math

import jax
import jax.numpy as jnp
import ml_dtypes
import numpy as np
from jax import lax
from jax.experimental import pallas as pl
from jax.experimental.pallas import tpu as pltpu
from jax.sharding import PartitionSpec as P

SAMPLES = 1024
NF = 256
BAND_LO = 16
EPSILON = 1e-06

SIDE = 4
OWNERS = SIDE * SIDE
SEG = 8
CH = 128
PAIRS = 1024
BINS = 8
ROWS = 2 * BINS
TILE = 256
TILES = PAIRS // TILE
QUADS = SEG // 2
EARLY = 2
MESH = pl.DeviceIdType.MESH


def basis_tables():
    sample_ids = np.arange(SAMPLES, dtype=np.int64)
    bin_ids = np.arange(NF, dtype=np.int64) + BAND_LO
    phases = bin_ids[:, None] * sample_ids[None, :] % SAMPLES
    step = np.float32(2.0 * math.pi / SAMPLES)
    angles = phases.astype(np.float32) * step
    tapers = np.float32(0.5) - np.float32(0.5) * np.cos(sample_ids.astype(np.float32) * step)
    table = np.stack([np.cos(angles) * tapers[None, :], -np.sin(angles) * tapers[None, :]])
    table = table.astype(np.float32).astype(ml_dtypes.bfloat16)
    table = table.reshape(2, SIDE, SIDE, 2, BINS, SAMPLES).transpose(3, 1, 2, 0, 4, 5)
    table = table.reshape(2, SIDE, SIDE, ROWS, SAMPLES)
    ids = np.arange(2 * SIDE - 1) % SIDE
    first = table[0][ids[None, :], (ids[:, None] + ids[None, :]) % SIDE]
    second = table[1][ids[:, None], ids[None, :]]
    return first, second


def kernel(
    basis_a_hbm, basis_b_hbm, rec_hbm, pair_hbm, live_hbm, out_ref,
    basis, rec, pair, live, w_left, w_right,
    own_a, near_a, far_a, stage_b, own_b, near_b, far_b, left_part, right_part, own_sum, send_sum, recv_sum, total_b,
    in_sem, za_send, za_recv, zb_send, zb_recv, gather_send, gather_recv, sum_send, sum_recv,
):
    t = lax.axis_index("tm")
    c = lax.axis_index("chan")
    n_chan = lax.axis_size("chan")
    y, x = lax.div(t, SIDE), lax.rem(t, SIDE)
    side = 1 - 2 * lax.rem(c, 2)
    c_near, c_far = c + side, c - side
    has_far = jnp.logical_and(c_far >= 0, c_far < n_chan)
    one_far = jnp.where(has_far, 1, 0)
    ways = ((0, near_a, near_b, c_near), (1, far_a, far_b, c_far))

    def on_way(way, act):
        if way == 0:
            act()
        else:
            pl.when(has_far)(act)

    def peer(dy, dx):
        return (lax.rem(y + dy, SIDE) * SIDE + lax.rem(x + dx, SIDE), c)

    others = [(dy, dx) for dy in (2, 1, 3, 0) for dx in (2, 1, 3, 0) if (dy, dx) != (0, 0)]

    barrier = pltpu.get_barrier_semaphore()
    for to in [peer(dy, dx) for dy, dx in others] + [(t, c_near)]:
        pl.semaphore_signal(barrier, inc=1, device_id=to, device_id_type=MESH)

    @pl.when(has_far)
    def _():
        pl.semaphore_signal(barrier, inc=1, device_id=(t, c_far), device_id_type=MESH)

    skew = lax.rem(x - y + SIDE, SIDE)
    basis_copies = [
        pltpu.make_async_copy(table.at[pl.ds(u, SIDE), pl.ds(v, SIDE)], basis.at[h], in_sem.at[2 + h])
        for h, (table, u, v) in enumerate(((basis_a_hbm, skew, y), (basis_b_hbm, y, x)))
    ]
    rec_copies = [
        pltpu.make_async_copy(rec_hbm.at[pl.ds(2 * q, 2)], rec.at[pl.ds(2 * q, 2)], in_sem.at[4 + q])
        for q in range(QUADS)
    ]
    pair_copy = pltpu.make_async_copy(pair_hbm, pair, in_sem.at[0])
    live_copy = pltpu.make_async_copy(live_hbm, live, in_sem.at[1])
    rec_copies[0].start()
    for copy in basis_copies:
        copy.start()
    for q in range(1, QUADS):
        rec_copies[q].start()
    pair_copy.start()
    live_copy.start()

    @pl.when(jnp.logical_not(has_far))
    def _():
        far_a[...] = jnp.zeros_like(far_a)
        far_b[...] = jnp.zeros_like(far_b)

    def make(source, landing, send_sem, recv_sem, to):
        return pltpu.make_async_remote_copy(
            src_ref=source,
            dst_ref=landing,
            send_sem=send_sem,
            recv_sem=recv_sem,
            device_id=to,
            device_id_type=MESH,
        )

    za, zb = [], []

    def send_z(copies, started=za):
        started.extend(copies)
        for way in (1, 0):
            @functools.partial(on_way, way)
            def _():
                for _, w, copy in copies:
                    if w == way:
                        copy.start()

    def wait_z(k, way, started=za):
        @functools.partial(on_way, way)
        def _():
            for part, w, copy in started:
                if part == k and w == way:
                    copy.wait()

    for copy in basis_copies:
        copy.wait()
    for q in range(QUADS):
        rec_copies[q].wait()
        wide = jnp.concatenate([rec[2 * q], rec[2 * q + 1]], axis=1)
        spectrum = jnp.dot(
            basis[...].reshape(2 * NF, SAMPLES), wide, preferred_element_type=jnp.float32
        )
        powers = jnp.sum(spectrum * spectrum, axis=0, keepdims=True) / NF
        white = (spectrum * lax.rsqrt(powers + EPSILON)).astype(jnp.bfloat16)
        for e in range(2):
            mine = white[:, e * CH:(e + 1) * CH].reshape(2, OWNERS, ROWS, CH)
            own_a[:, :, 2 * q + e] = mine[0].reshape(SIDE, SIDE, ROWS, CH)
            stage_b[q, :, e] = mine[1]
            own_b[q, 0, e] = mine[1, 0]
        if q == 0:
            continue
        if q == 1:
            pl.semaphore_wait(barrier, 1 + one_far + len(others))
        ready = (0, 1) if q == 1 else (q,)
        for k in range(EARLY):
            piece = (k, pl.ds(0, SIDE), pl.ds(2 * ready[0], 2 * len(ready)))
            sem = k * QUADS + q
            send_z([
                (k, way, make(own_a.at[piece], landing.at[piece], za_send.at[way, sem], za_recv.at[way, sem], (t, to)))
                for way, landing, _, to in ways
            ])
        for p in ready:
            for dy, dx in others:
                d = dy * SIDE + dx
                make(
                    stage_b.at[p, d], own_b.at[p, d], gather_send.at[p], gather_recv.at[p], peer(dy, dx)
                ).start()
    for k in range(EARLY, SIDE):
        sem = QUADS * EARLY + k - EARLY
        send_z([
            (k, way, make(own_a.at[k], landing.at[k], za_send.at[way, sem], za_recv.at[way, sem], (t, to)))
            for way, landing, _, to in ways
        ])

    pair_copy.wait()
    live_copy.wait()
    n_live = live[0]
    for n in range(TILES):
        cols = pl.ds(n * TILE, TILE)
        left = pair[0:1, cols] - c * CH
        right = pair[1:2, cols] - (c - 1) * CH
        slots = lax.broadcasted_iota(jnp.int32, (1, TILE), 1) + n * TILE
        left = jnp.where(slots < n_live, left, -1)
        ids = lax.broadcasted_iota(jnp.int32, (CH, TILE), 0)
        w_left[n] = jnp.where(ids == left, 1.0 / 128.0, 0.0).astype(jnp.bfloat16)
        for place, block in ((0, 1), (1, 1 + side), (2, 1 - side)):
            hot = jnp.where(ids + block * CH == right, 1.0, 0.0)
            w_right[n, pl.ds(place * CH, CH)] = hot.astype(jnp.bfloat16)

    def tile(n):
        return pl.ds(n * TILE, TILE)

    def before(own, near):
        mine = own.reshape(-1, CH)
        wide = jnp.concatenate([mine, near.reshape(-1, CH)], axis=1)
        for n in range(TILES):
            left_part[n] = jnp.dot(mine, w_left[n], preferred_element_type=jnp.float32)
            right_part[n] = jnp.dot(wide, w_right[n, :2 * CH], preferred_element_type=jnp.float32)

    def after(far, groups):
        far = far.reshape(-1, CH)
        shape = (groups, far.shape[0] // (groups * ROWS), 2, BINS, TILE)
        sums = []
        for n in range(TILES):
            left = left_part[n].reshape(shape)
            right = right_part[n] + jnp.dot(
                far, w_right[n, 2 * CH:], preferred_element_type=jnp.float32
            )
            right = right.reshape(shape)
            real = jnp.sum(left[:, :, 0] * right[:, :, 0] + left[:, :, 1] * right[:, :, 1], axis=1)
            imag = jnp.sum(left[:, :, 1] * right[:, :, 0] - left[:, :, 0] * right[:, :, 1], axis=1)
            sums.append(jnp.concatenate([real, imag], axis=1))
        return sums

    def before_a(k):
        wait_z(k, 0)
        before(own_a[k], near_a[k])

    def after_a(k):
        wait_z(k, 1)
        for n, both in enumerate(after(far_a[k], SIDE)):
            if k == 0:
                own_sum[:, tile(n)] = both[0]
            send_sum[k, :, :, tile(n)] = both.astype(jnp.bfloat16)
        for i in range(SIDE):
            dx = (i + k) % SIDE
            if (i, dx) != (0, 0):
                make(
                    send_sum.at[k, i], recv_sum.at[k, i], sum_send.at[k], sum_recv.at[k], peer(i, dx)
                ).start()

    def wait_bytes(ref, sem):
        pltpu.make_async_copy(ref, ref, sem).wait()

    def forward_b(q):
        wait_bytes(own_b.at[q, pl.ds(1, OWNERS - 1)], gather_recv.at[q])
        send_z([
            (q, way, make(own_b.at[q], landing.at[q], zb_send.at[way, q], zb_recv.at[way, q], (t, to)))
            for way, _, landing, to in ways
        ], zb)

    def before_b(q):
        wait_z(q, 0, zb)
        before(own_b[q], near_b[q])

    def after_b(q):
        wait_z(q, 1, zb)
        for n, both in enumerate(after(far_b[q], 1)):
            if q == 0:
                total_b[:, tile(n)] = both[0]
            elif q < QUADS - 1:
                total_b[:, tile(n)] += both[0]
            else:
                total = total_b[:, tile(n)] + both[0]
                out_ref[0, BINS:, tile(n)] = total[:BINS]
                out_ref[1, BINS:, tile(n)] = total[BINS:]

    def add_sums(k):
        lowest = 1 if k == 0 else 0
        wait_bytes(recv_sum.at[k, pl.ds(lowest, SIDE - lowest)], sum_recv.at[k])
        total = own_sum[...]
        for i in range(lowest, SIDE):
            total = total + recv_sum[k, i].astype(jnp.float32)
        if k < SIDE - 1:
            own_sum[...] = total
        else:
            out_ref[0, :BINS] = total[:BINS]
            out_ref[1, :BINS] = total[BINS:]

    before_a(0)
    after_a(0)
    before_a(1)
    forward_b(0)
    after_a(1)
    before_a(2)
    forward_b(1)
    after_a(2)
    before_a(3)
    forward_b(2)
    after_a(3)
    before_b(0)
    forward_b(3)
    after_b(0)
    before_b(1)
    after_b(1)
    add_sums(0)
    before_b(2)
    after_b(2)
    add_sums(1)
    before_b(3)
    add_sums(2)
    after_b(3)
    add_sums(3)
    for q in range(QUADS):
        wait_bytes(stage_b.at[q, pl.ds(1, OWNERS - 1)], gather_send.at[q])
    for k in range(SIDE):
        lowest = 1 if k == 0 else 0
        wait_bytes(send_sum.at[k, pl.ds(lowest, SIDE - lowest)], sum_send.at[k])


def body(records, pair_list, live_count):
    tables = [jnp.asarray(table) for table in basis_tables()]
    any_space = pl.BlockSpec(memory_space=pl.ANY)
    vmem, bf16, f32 = pltpu.VMEM, jnp.bfloat16, jnp.float32
    dma = pltpu.SemaphoreType.DMA
    block_a = vmem((SIDE, SIDE, SEG, ROWS, CH), bf16)
    block_b = vmem((QUADS, OWNERS, 2, ROWS, CH), bf16)
    parts = vmem((TILES, SIDE * SEG * ROWS, TILE), f32)
    return pl.pallas_call(
        kernel,
        out_shape=vmem((2, 2 * BINS, PAIRS), f32),
        in_specs=[any_space] * 5,
        out_specs=pl.BlockSpec(memory_space=vmem),
        scratch_shapes=[
            vmem((2, SIDE, SIDE, ROWS, SAMPLES), bf16),
            vmem((SEG, SAMPLES, CH), bf16),
            vmem((2, PAIRS), jnp.int32),
            pltpu.SMEM((1,), jnp.int32),
            vmem((TILES, CH, TILE), bf16),
            vmem((TILES, 3 * CH, TILE), bf16),
            block_a,
            block_a,
            block_a,
            block_b,
            block_b,
            block_b,
            block_b,
            parts,
            parts,
            vmem((ROWS, PAIRS), f32),
            vmem((SIDE, SIDE, ROWS, PAIRS), bf16),
            vmem((SIDE, SIDE, ROWS, PAIRS), bf16),
            vmem((ROWS, PAIRS), f32),
            dma((4 + QUADS,)),
            dma((2, QUADS * EARLY + SIDE - EARLY)),
            dma((2, QUADS * EARLY + SIDE - EARLY)),
            dma((2, QUADS)),
            dma((2, QUADS)),
            dma((QUADS,)),
            dma((QUADS,)),
            dma((SIDE,)),
            dma((SIDE,)),
        ],
        compiler_params=pltpu.CompilerParams(
            collective_id=0, has_side_effects=True, vmem_limit_bytes=56 * 2**20
        ),
        cost_estimate=pl.CostEstimate(
            flops=7 * 10**9, bytes_accessed=4 * 2**20, transcendentals=0
        ),
    )(*tables, records, pair_list, live_count)


def solution(mesh):
    in_specs = (P("tm", None, "chan"), P(None, "chan"), P("chan"))
    out_specs = P(None, "tm", "chan")
    return jax.shard_map(body, mesh=mesh, in_specs=in_specs, out_specs=out_specs, check_vma=False)
```

```python
import functools
import math

import jax
import jax.numpy as jnp
import ml_dtypes
import numpy as np
from jax import lax
from jax.experimental import pallas as pl
from jax.experimental.pallas import tpu as pltpu
from jax.sharding import PartitionSpec as P

SAMPLES = 1024
NF = 256
BAND_LO = 16
EPSILON = 1e-06

SIDE = 4
OWNERS = SIDE * SIDE
SEG = 8
CH = 128
PAIRS = 1024
BINS = 8
ROWS = 2 * BINS
TILE = 256
TILES = PAIRS // TILE
QUADS = SEG // 2
EARLY = 2
MESH = pl.DeviceIdType.MESH


def basis_tables():
    sample_ids = np.arange(SAMPLES, dtype=np.int64)
    bin_ids = np.arange(NF, dtype=np.int64) + BAND_LO
    phases = bin_ids[:, None] * sample_ids[None, :] % SAMPLES
    step = np.float32(2.0 * math.pi / SAMPLES)
    angles = phases.astype(np.float32) * step
    tapers = np.float32(0.5) - np.float32(0.5) * np.cos(sample_ids.astype(np.float32) * step)
    table = np.stack([np.cos(angles) * tapers[None, :], -np.sin(angles) * tapers[None, :]])
    table = table.astype(np.float32).astype(ml_dtypes.bfloat16)
    table = table.reshape(2, SIDE, SIDE, 2, BINS, SAMPLES).transpose(3, 1, 2, 0, 4, 5)
    table = table.reshape(2, SIDE, SIDE, ROWS, SAMPLES)
    ids = np.arange(2 * SIDE - 1) % SIDE
    first = table[0][ids[None, :], (ids[:, None] + ids[None, :]) % SIDE]
    second = table[1][ids[:, None], ids[None, :]]
    return first, second


def kernel(
    basis_a_hbm, basis_b_hbm, rec_hbm, pair_hbm, live_hbm, out_ref,
    basis, rec, pair, live, w_left, w_right,
    own_a, near_a, far_a, stage_b, own_b, near_b, far_b, left_part, right_part, own_sum, send_sum, recv_sum, total_b,
    in_sem, za_send, za_recv, zb_send, zb_recv, gather_send, gather_recv, sum_send, sum_recv,
):
    t = lax.axis_index("tm")
    c = lax.axis_index("chan")
    n_chan = lax.axis_size("chan")
    y, x = lax.div(t, SIDE), lax.rem(t, SIDE)
    side = 1 - 2 * lax.rem(c, 2)
    c_near, c_far = c + side, c - side
    has_far = jnp.logical_and(c_far >= 0, c_far < n_chan)
    one_far = jnp.where(has_far, 1, 0)
    ways = ((0, near_a, near_b, c_near), (1, far_a, far_b, c_far))

    def on_way(way, act):
        if way == 0:
            act()
        else:
            pl.when(has_far)(act)

    def peer(dy, dx):
        return (lax.rem(y + dy, SIDE) * SIDE + lax.rem(x + dx, SIDE), c)

    others = [(dy, dx) for dy in (2, 1, 3, 0) for dx in (2, 1, 3, 0) if (dy, dx) != (0, 0)]

    barrier = pltpu.get_barrier_semaphore()
    for to in [peer(dy, dx) for dy, dx in others] + [(t, c_near)]:
        pl.semaphore_signal(barrier, inc=1, device_id=to, device_id_type=MESH)

    @pl.when(has_far)
    def _():
        pl.semaphore_signal(barrier, inc=1, device_id=(t, c_far), device_id_type=MESH)

    skew = lax.rem(x - y + SIDE, SIDE)
    basis_copies = [
        pltpu.make_async_copy(table.at[pl.ds(u, SIDE), pl.ds(v, SIDE)], basis.at[h], in_sem.at[2 + h])
        for h, (table, u, v) in enumerate(((basis_a_hbm, skew, y), (basis_b_hbm, y, x)))
    ]
    rec_copies = [
        pltpu.make_async_copy(rec_hbm.at[pl.ds(2 * q, 2)], rec.at[pl.ds(2 * q, 2)], in_sem.at[4 + q])
        for q in range(QUADS)
    ]
    pair_copy = pltpu.make_async_copy(pair_hbm, pair, in_sem.at[0])
    live_copy = pltpu.make_async_copy(live_hbm, live, in_sem.at[1])
    rec_copies[0].start()
    for copy in basis_copies:
        copy.start()
    for q in range(1, QUADS):
        rec_copies[q].start()
    pair_copy.start()
    live_copy.start()

    @pl.when(jnp.logical_not(has_far))
    def _():
        far_a[...] = jnp.zeros_like(far_a)
        far_b[...] = jnp.zeros_like(far_b)

    def make(source, landing, send_sem, recv_sem, to):
        return pltpu.make_async_remote_copy(
            src_ref=source,
            dst_ref=landing,
            send_sem=send_sem,
            recv_sem=recv_sem,
            device_id=to,
            device_id_type=MESH,
        )

    za, zb = [], []

    def send_z(copies, started=za):
        started.extend(copies)
        for way in (1, 0):
            @functools.partial(on_way, way)
            def _():
                for _, w, copy in copies:
                    if w == way:
                        copy.start()

    def wait_z(k, way, started=za):
        @functools.partial(on_way, way)
        def _():
            for part, w, copy in started:
                if part == k and w == way:
                    copy.wait()

    for copy in basis_copies:
        copy.wait()
    for q in range(QUADS):
        rec_copies[q].wait()
        wide = jnp.concatenate([rec[2 * q], rec[2 * q + 1]], axis=1)
        spectrum = jnp.dot(
            basis[...].reshape(2 * NF, SAMPLES), wide, preferred_element_type=jnp.float32
        )
        powers = jnp.sum(spectrum * spectrum, axis=0, keepdims=True) / NF
        white = (spectrum * lax.rsqrt(powers + EPSILON)).astype(jnp.bfloat16)
        for e in range(2):
            mine = white[:, e * CH:(e + 1) * CH].reshape(2, OWNERS, ROWS, CH)
            own_a[:, :, 2 * q + e] = mine[0].reshape(SIDE, SIDE, ROWS, CH)
            stage_b[q, :, e] = mine[1]
            own_b[q, 0, e] = mine[1, 0]
        if q == 0:
            continue
        if q == 1:
            pl.semaphore_wait(barrier, 1 + one_far + len(others))
        ready = (0, 1) if q == 1 else (q,)
        for k in range(EARLY):
            piece = (k, pl.ds(0, SIDE), pl.ds(2 * ready[0], 2 * len(ready)))
            sem = k * QUADS + q
            send_z([
                (k, way, make(own_a.at[piece], landing.at[piece], za_send.at[way, sem], za_recv.at[way, sem], (t, to)))
                for way, landing, _, to in ways
            ])
        for p in ready:
            for dy, dx in others:
                d = dy * SIDE + dx
                make(
                    stage_b.at[p, d], own_b.at[p, d], gather_send.at[p], gather_recv.at[p], peer(dy, dx)
                ).start()
    for k in range(EARLY, SIDE):
        sem = QUADS * EARLY + k - EARLY
        send_z([
            (k, way, make(own_a.at[k], landing.at[k], za_send.at[way, sem], za_recv.at[way, sem], (t, to)))
            for way, landing, _, to in ways
        ])

    pair_copy.wait()
    live_copy.wait()
    n_live = live[0]
    for n in range(TILES):
        cols = pl.ds(n * TILE, TILE)
        left = pair[0:1, cols] - c * CH
        right = pair[1:2, cols] - (c - 1) * CH
        slots = lax.broadcasted_iota(jnp.int32, (1, TILE), 1) + n * TILE
        left = jnp.where(slots < n_live, left, -1)
        ids = lax.broadcasted_iota(jnp.int32, (CH, TILE), 0)
        w_left[n] = jnp.where(ids == left, 1.0 / 128.0, 0.0).astype(jnp.bfloat16)
        for place, block in ((0, 1), (1, 1 + side), (2, 1 - side)):
            hot = jnp.where(ids + block * CH == right, 1.0, 0.0)
            w_right[n, pl.ds(place * CH, CH)] = hot.astype(jnp.bfloat16)

    def tile(n):
        return pl.ds(n * TILE, TILE)

    def before(own, near):
        mine = own.reshape(-1, CH)
        wide = jnp.concatenate([mine, near.reshape(-1, CH)], axis=1)
        for n in range(TILES):
            left_part[n] = jnp.dot(mine, w_left[n], preferred_element_type=jnp.float32)
            right_part[n] = jnp.dot(wide, w_right[n, :2 * CH], preferred_element_type=jnp.float32)

    def after(far, groups):
        far = far.reshape(-1, CH)
        shape = (groups, far.shape[0] // (groups * ROWS), 2, BINS, TILE)
        sums = []
        for n in range(TILES):
            left = left_part[n].reshape(shape)
            right = right_part[n] + jnp.dot(
                far, w_right[n, 2 * CH:], preferred_element_type=jnp.float32
            )
            right = right.reshape(shape)
            real = jnp.sum(left[:, :, 0] * right[:, :, 0] + left[:, :, 1] * right[:, :, 1], axis=1)
            imag = jnp.sum(left[:, :, 1] * right[:, :, 0] - left[:, :, 0] * right[:, :, 1], axis=1)
            sums.append(jnp.concatenate([real, imag], axis=1))
        return sums

    def before_a(k):
        wait_z(k, 0)
        before(own_a[k], near_a[k])

    def after_a(k):
        wait_z(k, 1)
        for n, both in enumerate(after(far_a[k], SIDE)):
            if k == 0:
                own_sum[:, tile(n)] = both[0]
            send_sum[k, :, :, tile(n)] = both.astype(jnp.bfloat16)
        for i in range(SIDE):
            dx = (i + k) % SIDE
            if (i, dx) != (0, 0):
                make(
                    send_sum.at[k, i], recv_sum.at[k, i], sum_send.at[k], sum_recv.at[k], peer(i, dx)
                ).start()

    def wait_bytes(ref, sem):
        pltpu.make_async_copy(ref, ref, sem).wait()

    def forward_b(q):
        wait_bytes(own_b.at[q, pl.ds(1, OWNERS - 1)], gather_recv.at[q])
        send_z([
            (q, way, make(own_b.at[q], landing.at[q], zb_send.at[way, q], zb_recv.at[way, q], (t, to)))
            for way, _, landing, to in ways
        ], zb)

    def before_b(q):
        wait_z(q, 0, zb)
        before(own_b[q], near_b[q])

    def after_b(q):
        wait_z(q, 1, zb)
        for n, both in enumerate(after(far_b[q], 1)):
            if q == 0:
                total_b[:, tile(n)] = both[0]
            elif q < QUADS - 1:
                total_b[:, tile(n)] += both[0]
            else:
                total = total_b[:, tile(n)] + both[0]
                out_ref[0, BINS:, tile(n)] = total[:BINS]
                out_ref[1, BINS:, tile(n)] = total[BINS:]

    def add_sums(k):
        lowest = 1 if k == 0 else 0
        wait_bytes(recv_sum.at[k, pl.ds(lowest, SIDE - lowest)], sum_recv.at[k])
        total = own_sum[...]
        for i in range(lowest, SIDE):
            total = total + recv_sum[k, i].astype(jnp.float32)
        if k < SIDE - 1:
            own_sum[...] = total
        else:
            out_ref[0, :BINS] = total[:BINS]
            out_ref[1, :BINS] = total[BINS:]

    for k in range(SIDE - 1):
        forward_b(k)
        before_a(k)
        after_a(k)
    before_a(SIDE - 1)
    after_a(SIDE - 1)
    forward_b(SIDE - 1)
    before_b(0)
    after_b(0)
    before_b(1)
    after_b(1)
    add_sums(0)
    before_b(2)
    after_b(2)
    add_sums(1)
    before_b(3)
    add_sums(2)
    after_b(3)
    add_sums(3)
    for q in range(QUADS):
        wait_bytes(stage_b.at[q, pl.ds(1, OWNERS - 1)], gather_send.at[q])
    for k in range(SIDE):
        lowest = 1 if k == 0 else 0
        wait_bytes(send_sum.at[k, pl.ds(lowest, SIDE - lowest)], sum_send.at[k])


def body(records, pair_list, live_count):
    tables = [jnp.asarray(table) for table in basis_tables()]
    any_space = pl.BlockSpec(memory_space=pl.ANY)
    vmem, bf16, f32 = pltpu.VMEM, jnp.bfloat16, jnp.float32
    dma = pltpu.SemaphoreType.DMA
    block_a = vmem((SIDE, SIDE, SEG, ROWS, CH), bf16)
    block_b = vmem((QUADS, OWNERS, 2, ROWS, CH), bf16)
    parts = vmem((TILES, SIDE * SEG * ROWS, TILE), f32)
    return pl.pallas_call(
        kernel,
        out_shape=vmem((2, 2 * BINS, PAIRS), f32),
        in_specs=[any_space] * 5,
        out_specs=pl.BlockSpec(memory_space=vmem),
        scratch_shapes=[
            vmem((2, SIDE, SIDE, ROWS, SAMPLES), bf16),
            vmem((SEG, SAMPLES, CH), bf16),
            vmem((2, PAIRS), jnp.int32),
            pltpu.SMEM((1,), jnp.int32),
            vmem((TILES, CH, TILE), bf16),
            vmem((TILES, 3 * CH, TILE), bf16),
            block_a,
            block_a,
            block_a,
            block_b,
            block_b,
            block_b,
            block_b,
            parts,
            parts,
            vmem((ROWS, PAIRS), f32),
            vmem((SIDE, SIDE, ROWS, PAIRS), bf16),
            vmem((SIDE, SIDE, ROWS, PAIRS), bf16),
            vmem((ROWS, PAIRS), f32),
            dma((4 + QUADS,)),
            dma((2, QUADS * EARLY + SIDE - EARLY)),
            dma((2, QUADS * EARLY + SIDE - EARLY)),
            dma((2, QUADS)),
            dma((2, QUADS)),
            dma((QUADS,)),
            dma((QUADS,)),
            dma((SIDE,)),
            dma((SIDE,)),
        ],
        compiler_params=pltpu.CompilerParams(
            collective_id=0, has_side_effects=True, vmem_limit_bytes=56 * 2**20
        ),
        cost_estimate=pl.CostEstimate(
            flops=7 * 10**9, bytes_accessed=4 * 2**20, transcendentals=0
        ),
    )(*tables, records, pair_list, live_count)


def solution(mesh):
    in_specs = (P("tm", None, "chan"), P(None, "chan"), P("chan"))
    out_specs = P(None, "tm", "chan")
    return jax.shard_map(body, mesh=mesh, in_specs=in_specs, out_specs=out_specs, check_vma=False)
```

```python
import functools
import math

import jax
import jax.numpy as jnp
import ml_dtypes
import numpy as np
from jax import lax
from jax.experimental import pallas as pl
from jax.experimental.pallas import tpu as pltpu
from jax.sharding import PartitionSpec as P

SAMPLES = 1024
NF = 256
BAND_LO = 16
EPSILON = 1e-06

SIDE = 4
OWNERS = SIDE * SIDE
SEG = 8
CH = 128
PAIRS = 1024
BINS = 8
ROWS = 2 * BINS
TILE = 256
TILES = PAIRS // TILE
QUADS = SEG // 2
EARLY = 2
PIECES = tuple((q, 0, OWNERS) for q in range(QUADS - 1)) + tuple(
    (QUADS - 1, h * OWNERS // 2, OWNERS // 2) for h in range(2)
)
MESH = pl.DeviceIdType.MESH


def basis_tables():
    sample_ids = np.arange(SAMPLES, dtype=np.int64)
    bin_ids = np.arange(NF, dtype=np.int64) + BAND_LO
    phases = bin_ids[:, None] * sample_ids[None, :] % SAMPLES
    step = np.float32(2.0 * math.pi / SAMPLES)
    angles = phases.astype(np.float32) * step
    tapers = np.float32(0.5) - np.float32(0.5) * np.cos(sample_ids.astype(np.float32) * step)
    table = np.stack([np.cos(angles) * tapers[None, :], -np.sin(angles) * tapers[None, :]])
    table = table.astype(np.float32).astype(ml_dtypes.bfloat16)
    table = table.reshape(2, SIDE, SIDE, 2, BINS, SAMPLES).transpose(3, 1, 2, 0, 4, 5)
    table = table.reshape(2, SIDE, SIDE, ROWS, SAMPLES)
    ids = np.arange(2 * SIDE - 1) % SIDE
    first = table[0][ids[None, :], (ids[:, None] + ids[None, :]) % SIDE]
    second = table[1][ids[:, None], ids[None, :]]
    return first, second


def kernel(
    basis_a_hbm, basis_b_hbm, rec_hbm, pair_hbm, live_hbm, out_ref,
    basis, rec, pair, live, w_left, w_right,
    own_a, near_a, far_a, stage_b, own_b, near_b, far_b, left_part, right_part, own_sum, send_sum, recv_sum, total_b,
    in_sem, za_send, za_recv, zb_send, zb_recv, gather_send, gather_recv, sum_send, sum_recv,
):
    t = lax.axis_index("tm")
    c = lax.axis_index("chan")
    n_chan = lax.axis_size("chan")
    y, x = lax.div(t, SIDE), lax.rem(t, SIDE)
    side = 1 - 2 * lax.rem(c, 2)
    c_near, c_far = c + side, c - side
    has_far = jnp.logical_and(c_far >= 0, c_far < n_chan)
    one_far = jnp.where(has_far, 1, 0)
    ways = ((0, near_a, near_b, c_near), (1, far_a, far_b, c_far))

    def on_way(way, act):
        if way == 0:
            act()
        else:
            pl.when(has_far)(act)

    def peer(dy, dx):
        return (lax.rem(y + dy, SIDE) * SIDE + lax.rem(x + dx, SIDE), c)

    others = [(dy, dx) for dy in (2, 1, 3, 0) for dx in (2, 1, 3, 0) if (dy, dx) != (0, 0)]

    barrier = pltpu.get_barrier_semaphore()
    for to in [peer(dy, dx) for dy, dx in others] + [(t, c_near)]:
        pl.semaphore_signal(barrier, inc=1, device_id=to, device_id_type=MESH)

    @pl.when(has_far)
    def _():
        pl.semaphore_signal(barrier, inc=1, device_id=(t, c_far), device_id_type=MESH)

    skew = lax.rem(x - y + SIDE, SIDE)
    basis_copies = [
        pltpu.make_async_copy(table.at[pl.ds(u, SIDE), pl.ds(v, SIDE)], basis.at[h], in_sem.at[2 + h])
        for h, (table, u, v) in enumerate(((basis_a_hbm, skew, y), (basis_b_hbm, y, x)))
    ]
    rec_copies = [
        pltpu.make_async_copy(rec_hbm.at[pl.ds(2 * q, 2)], rec.at[pl.ds(2 * q, 2)], in_sem.at[4 + q])
        for q in range(QUADS)
    ]
    pair_copy = pltpu.make_async_copy(pair_hbm, pair, in_sem.at[0])
    live_copy = pltpu.make_async_copy(live_hbm, live, in_sem.at[1])
    rec_copies[0].start()
    for copy in basis_copies:
        copy.start()
    for q in range(1, QUADS):
        rec_copies[q].start()
    pair_copy.start()
    live_copy.start()

    @pl.when(jnp.logical_not(has_far))
    def _():
        far_a[...] = jnp.zeros_like(far_a)
        far_b[...] = jnp.zeros_like(far_b)

    def make(source, landing, send_sem, recv_sem, to):
        return pltpu.make_async_remote_copy(
            src_ref=source,
            dst_ref=landing,
            send_sem=send_sem,
            recv_sem=recv_sem,
            device_id=to,
            device_id_type=MESH,
        )

    za, zb = [], []

    def send_z(copies, started=za):
        started.extend(copies)
        for way in (1, 0):
            @functools.partial(on_way, way)
            def _():
                for _, w, copy in copies:
                    if w == way:
                        copy.start()

    def wait_z(k, way, started=za):
        @functools.partial(on_way, way)
        def _():
            for part, w, copy in started:
                if part == k and w == way:
                    copy.wait()

    for copy in basis_copies:
        copy.wait()
    for q in range(QUADS):
        rec_copies[q].wait()
        wide = jnp.concatenate([rec[2 * q], rec[2 * q + 1]], axis=1)
        spectrum = jnp.dot(
            basis[...].reshape(2 * NF, SAMPLES), wide, preferred_element_type=jnp.float32
        )
        powers = jnp.sum(spectrum * spectrum, axis=0, keepdims=True) / NF
        white = (spectrum * lax.rsqrt(powers + EPSILON)).astype(jnp.bfloat16)
        for e in range(2):
            mine = white[:, e * CH:(e + 1) * CH].reshape(2, OWNERS, ROWS, CH)
            own_a[:, :, 2 * q + e] = mine[0].reshape(SIDE, SIDE, ROWS, CH)
            stage_b[q, :, e] = mine[1]
            own_b[q, 0, e] = mine[1, 0]
        if q == 0:
            continue
        if q == 1:
            pl.semaphore_wait(barrier, 1 + one_far + len(others))
        ready = (0, 1) if q == 1 else (q,)
        for k in range(EARLY):
            piece = (k, pl.ds(0, SIDE), pl.ds(2 * ready[0], 2 * len(ready)))
            sem = k * QUADS + q
            send_z([
                (k, way, make(own_a.at[piece], landing.at[piece], za_send.at[way, sem], za_recv.at[way, sem], (t, to)))
                for way, landing, _, to in ways
            ])
        for p in ready:
            for dy, dx in others:
                d = dy * SIDE + dx
                make(
                    stage_b.at[p, d], own_b.at[p, d], gather_send.at[p], gather_recv.at[p], peer(dy, dx)
                ).start()
    for k in range(EARLY, SIDE):
        sem = QUADS * EARLY + k - EARLY
        send_z([
            (k, way, make(own_a.at[k], landing.at[k], za_send.at[way, sem], za_recv.at[way, sem], (t, to)))
            for way, landing, _, to in ways
        ])

    pair_copy.wait()
    live_copy.wait()
    n_live = live[0]
    for n in range(TILES):
        cols = pl.ds(n * TILE, TILE)
        left = pair[0:1, cols] - c * CH
        right = pair[1:2, cols] - (c - 1) * CH
        slots = lax.broadcasted_iota(jnp.int32, (1, TILE), 1) + n * TILE
        left = jnp.where(slots < n_live, left, -1)
        ids = lax.broadcasted_iota(jnp.int32, (CH, TILE), 0)
        w_left[n] = jnp.where(ids == left, 1.0 / 128.0, 0.0).astype(jnp.bfloat16)
        for place, block in ((0, 1), (1, 1 + side), (2, 1 - side)):
            hot = jnp.where(ids + block * CH == right, 1.0, 0.0)
            w_right[n, pl.ds(place * CH, CH)] = hot.astype(jnp.bfloat16)

    def tile(n):
        return pl.ds(n * TILE, TILE)

    def before(own, near):
        mine = own.reshape(-1, CH)
        wide = jnp.concatenate([mine, near.reshape(-1, CH)], axis=1)
        rows = pl.ds(0, mine.shape[0])
        for n in range(TILES):
            left_part[n, rows] = jnp.dot(mine, w_left[n], preferred_element_type=jnp.float32)
            right_part[n, rows] = jnp.dot(
                wide, w_right[n, :2 * CH], preferred_element_type=jnp.float32
            )

    def after(far, groups):
        far = far.reshape(-1, CH)
        rows = pl.ds(0, far.shape[0])
        shape = (groups, far.shape[0] // (groups * ROWS), 2, BINS, TILE)
        sums = []
        for n in range(TILES):
            left = left_part[n, rows].reshape(shape)
            right = right_part[n, rows] + jnp.dot(
                far, w_right[n, 2 * CH:], preferred_element_type=jnp.float32
            )
            right = right.reshape(shape)
            real = jnp.sum(left[:, :, 0] * right[:, :, 0] + left[:, :, 1] * right[:, :, 1], axis=1)
            imag = jnp.sum(left[:, :, 1] * right[:, :, 0] - left[:, :, 0] * right[:, :, 1], axis=1)
            sums.append(jnp.concatenate([real, imag], axis=1))
        return sums

    def before_a(k):
        wait_z(k, 0)
        before(own_a[k], near_a[k])

    def after_a(k):
        wait_z(k, 1)
        for n, both in enumerate(after(far_a[k], SIDE)):
            if k == 0:
                own_sum[:, tile(n)] = both[0]
            send_sum[k, :, :, tile(n)] = both.astype(jnp.bfloat16)
        for i in range(SIDE):
            dx = (i + k) % SIDE
            if (i, dx) != (0, 0):
                make(
                    send_sum.at[k, i], recv_sum.at[k, i], sum_send.at[k], sum_recv.at[k], peer(i, dx)
                ).start()

    def wait_bytes(ref, sem):
        pltpu.make_async_copy(ref, ref, sem).wait()

    def forward_b(q):
        wait_bytes(own_b.at[q, pl.ds(1, OWNERS - 1)], gather_recv.at[q])
        for p, (pair_id, source, count) in enumerate(PIECES):
            if pair_id == q:
                piece = (q, pl.ds(source, count))
                send_z([
                    (p, way, make(own_b.at[piece], landing.at[piece], zb_send.at[way, p], zb_recv.at[way, p], (t, to)))
                    for way, _, landing, to in ways
                ], zb)

    def before_b(p):
        wait_z(p, 0, zb)
        q, source, count = PIECES[p]
        before(own_b[q, source:source + count], near_b[q, source:source + count])

    def after_b(p):
        wait_z(p, 1, zb)
        q, source, count = PIECES[p]
        for n, both in enumerate(after(far_b[q, source:source + count], 1)):
            if p == 0:
                total_b[:, tile(n)] = both[0]
            elif p < len(PIECES) - 1:
                total_b[:, tile(n)] += both[0]
            else:
                total = total_b[:, tile(n)] + both[0]
                out_ref[0, BINS:, tile(n)] = total[:BINS]
                out_ref[1, BINS:, tile(n)] = total[BINS:]

    def add_sums(k):
        lowest = 1 if k == 0 else 0
        wait_bytes(recv_sum.at[k, pl.ds(lowest, SIDE - lowest)], sum_recv.at[k])
        total = own_sum[...]
        for i in range(lowest, SIDE):
            total = total + recv_sum[k, i].astype(jnp.float32)
        if k < SIDE - 1:
            own_sum[...] = total
        else:
            out_ref[0, :BINS] = total[:BINS]
            out_ref[1, :BINS] = total[BINS:]

    before_a(0)
    after_a(0)
    before_a(1)
    forward_b(0)
    after_a(1)
    before_a(2)
    forward_b(1)
    after_a(2)
    before_a(3)
    forward_b(2)
    after_a(3)
    before_b(0)
    forward_b(3)
    after_b(0)
    before_b(1)
    after_b(1)
    add_sums(0)
    before_b(2)
    after_b(2)
    add_sums(1)
    before_b(3)
    add_sums(2)
    after_b(3)
    before_b(4)
    after_b(4)
    add_sums(3)
    for q in range(QUADS):
        wait_bytes(stage_b.at[q, pl.ds(1, OWNERS - 1)], gather_send.at[q])
    for k in range(SIDE):
        lowest = 1 if k == 0 else 0
        wait_bytes(send_sum.at[k, pl.ds(lowest, SIDE - lowest)], sum_send.at[k])


def body(records, pair_list, live_count):
    tables = [jnp.asarray(table) for table in basis_tables()]
    any_space = pl.BlockSpec(memory_space=pl.ANY)
    vmem, bf16, f32 = pltpu.VMEM, jnp.bfloat16, jnp.float32
    dma = pltpu.SemaphoreType.DMA
    block_a = vmem((SIDE, SIDE, SEG, ROWS, CH), bf16)
    block_b = vmem((QUADS, OWNERS, 2, ROWS, CH), bf16)
    parts = vmem((TILES, SIDE * SEG * ROWS, TILE), f32)
    return pl.pallas_call(
        kernel,
        out_shape=vmem((2, 2 * BINS, PAIRS), f32),
        in_specs=[any_space] * 5,
        out_specs=pl.BlockSpec(memory_space=vmem),
        scratch_shapes=[
            vmem((2, SIDE, SIDE, ROWS, SAMPLES), bf16),
            vmem((SEG, SAMPLES, CH), bf16),
            vmem((2, PAIRS), jnp.int32),
            pltpu.SMEM((1,), jnp.int32),
            vmem((TILES, CH, TILE), bf16),
            vmem((TILES, 3 * CH, TILE), bf16),
            block_a,
            block_a,
            block_a,
            block_b,
            block_b,
            block_b,
            block_b,
            parts,
            parts,
            vmem((ROWS, PAIRS), f32),
            vmem((SIDE, SIDE, ROWS, PAIRS), bf16),
            vmem((SIDE, SIDE, ROWS, PAIRS), bf16),
            vmem((ROWS, PAIRS), f32),
            dma((4 + QUADS,)),
            dma((2, QUADS * EARLY + SIDE - EARLY)),
            dma((2, QUADS * EARLY + SIDE - EARLY)),
            dma((2, len(PIECES))),
            dma((2, len(PIECES))),
            dma((QUADS,)),
            dma((QUADS,)),
            dma((SIDE,)),
            dma((SIDE,)),
        ],
        compiler_params=pltpu.CompilerParams(
            collective_id=0, has_side_effects=True, vmem_limit_bytes=56 * 2**20
        ),
        cost_estimate=pl.CostEstimate(
            flops=7 * 10**9, bytes_accessed=4 * 2**20, transcendentals=0
        ),
    )(*tables, records, pair_list, live_count)


def solution(mesh):
    in_specs = (P("tm", None, "chan"), P(None, "chan"), P("chan"))
    out_specs = P(None, "tm", "chan")
    return jax.shard_map(body, mesh=mesh, in_specs=in_specs, out_specs=out_specs, check_vma=False)
```

```python
import functools
import math

import jax
import jax.numpy as jnp
import ml_dtypes
import numpy as np
from jax import lax
from jax.experimental import pallas as pl
from jax.experimental.pallas import tpu as pltpu
from jax.sharding import PartitionSpec as P

SAMPLES = 1024
NF = 256
BAND_LO = 16
EPSILON = 1e-06

SIDE = 4
OWNERS = SIDE * SIDE
SEG = 8
CH = 128
PAIRS = 1024
BINS = 8
ROWS = 2 * BINS
TILE = 256
TILES = PAIRS // TILE
QUADS = SEG // 2
EARLY = 2
MESH = pl.DeviceIdType.MESH


def basis_tables():
    sample_ids = np.arange(SAMPLES, dtype=np.int64)
    bin_ids = np.arange(NF, dtype=np.int64) + BAND_LO
    phases = bin_ids[:, None] * sample_ids[None, :] % SAMPLES
    step = np.float32(2.0 * math.pi / SAMPLES)
    angles = phases.astype(np.float32) * step
    tapers = np.float32(0.5) - np.float32(0.5) * np.cos(sample_ids.astype(np.float32) * step)
    table = np.stack([np.cos(angles) * tapers[None, :], -np.sin(angles) * tapers[None, :]])
    table = table.astype(np.float32).astype(ml_dtypes.bfloat16)
    table = table.reshape(2, SIDE, SIDE, 2, BINS, SAMPLES).transpose(3, 1, 2, 0, 4, 5)
    table = table.reshape(2, SIDE, SIDE, ROWS, SAMPLES)
    ids = np.arange(2 * SIDE - 1) % SIDE
    first = table[0][ids[None, :], (ids[:, None] + ids[None, :]) % SIDE]
    second = table[1][ids[:, None], ids[None, :]]
    return first, second


def kernel(
    basis_a_hbm, basis_b_hbm, rec_hbm, pair_hbm, live_hbm, out_ref,
    basis, rec, pair, live, w_left, w_right,
    own_a, near_a, far_a, stage_b, own_b, near_b, far_b, left_part, right_part, own_sum, send_sum, recv_sum, total_b,
    in_sem, za_send, za_recv, zb_send, zb_recv, gather_send, gather_recv, sum_send, sum_recv,
):
    t = lax.axis_index("tm")
    c = lax.axis_index("chan")
    n_chan = lax.axis_size("chan")
    y, x = lax.div(t, SIDE), lax.rem(t, SIDE)
    side = 1 - 2 * lax.rem(c, 2)
    c_near, c_far = c + side, c - side
    has_far = jnp.logical_and(c_far >= 0, c_far < n_chan)
    one_far = jnp.where(has_far, 1, 0)
    ways = ((0, near_a, near_b, c_near), (1, far_a, far_b, c_far))

    def on_way(way, act):
        if way == 0:
            act()
        else:
            pl.when(has_far)(act)

    def peer(dy, dx):
        return (lax.rem(y + dy, SIDE) * SIDE + lax.rem(x + dx, SIDE), c)

    others = [(dy, dx) for dy in (2, 1, 3, 0) for dx in (2, 1, 3, 0) if (dy, dx) != (0, 0)]

    barrier = pltpu.get_barrier_semaphore()
    for to in [peer(dy, dx) for dy, dx in others] + [(t, c_near)]:
        pl.semaphore_signal(barrier, inc=1, device_id=to, device_id_type=MESH)

    @pl.when(has_far)
    def _():
        pl.semaphore_signal(barrier, inc=1, device_id=(t, c_far), device_id_type=MESH)

    skew = lax.rem(x - y + SIDE, SIDE)
    basis_copies = [
        pltpu.make_async_copy(table.at[pl.ds(u, SIDE), pl.ds(v, SIDE)], basis.at[h], in_sem.at[2 + h])
        for h, (table, u, v) in enumerate(((basis_a_hbm, skew, y), (basis_b_hbm, y, x)))
    ]
    rec_copies = [
        pltpu.make_async_copy(rec_hbm.at[pl.ds(2 * q, 2)], rec.at[pl.ds(2 * q, 2)], in_sem.at[4 + q])
        for q in range(QUADS)
    ]
    pair_copy = pltpu.make_async_copy(pair_hbm, pair, in_sem.at[0])
    live_copy = pltpu.make_async_copy(live_hbm, live, in_sem.at[1])
    rec_copies[0].start()
    for copy in basis_copies:
        copy.start()
    for q in range(1, QUADS):
        rec_copies[q].start()
    pair_copy.start()
    live_copy.start()

    @pl.when(jnp.logical_not(has_far))
    def _():
        far_a[...] = jnp.zeros_like(far_a)
        far_b[...] = jnp.zeros_like(far_b)

    def make(source, landing, send_sem, recv_sem, to):
        return pltpu.make_async_remote_copy(
            src_ref=source,
            dst_ref=landing,
            send_sem=send_sem,
            recv_sem=recv_sem,
            device_id=to,
            device_id_type=MESH,
        )

    za, zb = [], []

    def send_z(copies, started=za):
        started.extend(copies)
        for way in (1, 0):
            @functools.partial(on_way, way)
            def _():
                for _, w, copy in copies:
                    if w == way:
                        copy.start()

    def wait_z(k, way, started=za):
        @functools.partial(on_way, way)
        def _():
            for part, w, copy in started:
                if part == k and w == way:
                    copy.wait()

    for copy in basis_copies:
        copy.wait()
    for q in range(QUADS):
        rec_copies[q].wait()
        wide = jnp.concatenate([rec[2 * q], rec[2 * q + 1]], axis=1)
        spectrum = jnp.dot(
            basis[...].reshape(2 * NF, SAMPLES), wide, preferred_element_type=jnp.float32
        )
        powers = jnp.sum(spectrum * spectrum, axis=0, keepdims=True) / NF
        white = (spectrum * lax.rsqrt(powers + EPSILON)).astype(jnp.bfloat16)
        for e in range(2):
            mine = white[:, e * CH:(e + 1) * CH].reshape(2, OWNERS, ROWS, CH)
            own_a[:, :, 2 * q + e] = mine[0].reshape(SIDE, SIDE, ROWS, CH)
            stage_b[q, :, e] = mine[1]
            own_b[q, 0, e] = mine[1, 0]
        if q == 0:
            pl.semaphore_wait(barrier, 1 + one_far + len(others))
        for k in range(EARLY):
            piece = (k, pl.ds(0, SIDE), pl.ds(2 * q, 2))
            sem = k * QUADS + q
            send_z([
                (k, way, make(own_a.at[piece], landing.at[piece], za_send.at[way, sem], za_recv.at[way, sem], (t, to)))
                for way, landing, _, to in ways
            ])
        for dy, dx in others:
            d = dy * SIDE + dx
            make(
                stage_b.at[q, d], own_b.at[q, d], gather_send.at[q], gather_recv.at[q], peer(dy, dx)
            ).start()
    for k in range(EARLY, SIDE):
        sem = QUADS * EARLY + k - EARLY
        send_z([
            (k, way, make(own_a.at[k], landing.at[k], za_send.at[way, sem], za_recv.at[way, sem], (t, to)))
            for way, landing, _, to in ways
        ])

    pair_copy.wait()
    live_copy.wait()
    n_live = live[0]
    for n in range(TILES):
        cols = pl.ds(n * TILE, TILE)
        left = pair[0:1, cols] - c * CH
        right = pair[1:2, cols] - (c - 1) * CH
        slots = lax.broadcasted_iota(jnp.int32, (1, TILE), 1) + n * TILE
        left = jnp.where(slots < n_live, left, -1)
        ids = lax.broadcasted_iota(jnp.int32, (CH, TILE), 0)
        w_left[n] = jnp.where(ids == left, 1.0 / 128.0, 0.0).astype(jnp.bfloat16)
        for place, block in ((0, 1), (1, 1 + side), (2, 1 - side)):
            hot = jnp.where(ids + block * CH == right, 1.0, 0.0)
            w_right[n, pl.ds(place * CH, CH)] = hot.astype(jnp.bfloat16)

    def tile(n):
        return pl.ds(n * TILE, TILE)

    def before(own, near):
        mine = own.reshape(-1, CH)
        wide = jnp.concatenate([mine, near.reshape(-1, CH)], axis=1)
        for n in range(TILES):
            left_part[n] = jnp.dot(mine, w_left[n], preferred_element_type=jnp.float32)
            right_part[n] = jnp.dot(wide, w_right[n, :2 * CH], preferred_element_type=jnp.float32)

    def after(far, groups):
        far = far.reshape(-1, CH)
        shape = (groups, far.shape[0] // (groups * ROWS), 2, BINS, TILE)
        sums = []
        for n in range(TILES):
            left = left_part[n].reshape(shape)
            right = right_part[n] + jnp.dot(
                far, w_right[n, 2 * CH:], preferred_element_type=jnp.float32
            )
            right = right.reshape(shape)
            real = jnp.sum(left[:, :, 0] * right[:, :, 0] + left[:, :, 1] * right[:, :, 1], axis=1)
            imag = jnp.sum(left[:, :, 1] * right[:, :, 0] - left[:, :, 0] * right[:, :, 1], axis=1)
            sums.append(jnp.concatenate([real, imag], axis=1))
        return sums

    def before_a(k):
        wait_z(k, 0)
        before(own_a[k], near_a[k])

    def after_a(k):
        wait_z(k, 1)
        for n, both in enumerate(after(far_a[k], SIDE)):
            if k == 0:
                own_sum[:, tile(n)] = both[0]
            send_sum[k, :, :, tile(n)] = both.astype(jnp.bfloat16)
        for i in range(SIDE):
            dx = (i + k) % SIDE
            if (i, dx) != (0, 0):
                make(
                    send_sum.at[k, i], recv_sum.at[k, i], sum_send.at[k], sum_recv.at[k], peer(i, dx)
                ).start()

    def wait_bytes(ref, sem):
        pltpu.make_async_copy(ref, ref, sem).wait()

    def forward_b(q):
        wait_bytes(own_b.at[q, pl.ds(1, OWNERS - 1)], gather_recv.at[q])
        send_z([
            (q, way, make(own_b.at[q], landing.at[q], zb_send.at[way, q], zb_recv.at[way, q], (t, to)))
            for way, _, landing, to in ways
        ], zb)

    def before_b(q):
        wait_z(q, 0, zb)
        before(own_b[q], near_b[q])

    def after_b(q):
        wait_z(q, 1, zb)
        for n, both in enumerate(after(far_b[q], 1)):
            if q == 0:
                total_b[:, tile(n)] = both[0]
            elif q < QUADS - 1:
                total_b[:, tile(n)] += both[0]
            else:
                total = total_b[:, tile(n)] + both[0]
                out_ref[0, BINS:, tile(n)] = total[:BINS]
                out_ref[1, BINS:, tile(n)] = total[BINS:]

    def add_sums(k):
        lowest = 1 if k == 0 else 0
        wait_bytes(recv_sum.at[k, pl.ds(lowest, SIDE - lowest)], sum_recv.at[k])
        total = own_sum[...]
        for i in range(lowest, SIDE):
            total = total + recv_sum[k, i].astype(jnp.float32)
        if k < SIDE - 1:
            own_sum[...] = total
        else:
            out_ref[0, :BINS] = total[:BINS]
            out_ref[1, :BINS] = total[BINS:]

    before_a(0)
    after_a(0)
    before_a(1)
    forward_b(0)
    after_a(1)
    before_a(2)
    forward_b(1)
    after_a(2)
    before_a(3)
    forward_b(2)
    after_a(3)
    forward_b(3)
    before_b(0)
    after_b(0)
    before_b(1)
    after_b(1)
    add_sums(0)
    before_b(2)
    after_b(2)
    add_sums(1)
    before_b(3)
    add_sums(2)
    after_b(3)
    add_sums(3)
    for q in range(QUADS):
        wait_bytes(stage_b.at[q, pl.ds(1, OWNERS - 1)], gather_send.at[q])
    for k in range(SIDE):
        lowest = 1 if k == 0 else 0
        wait_bytes(send_sum.at[k, pl.ds(lowest, SIDE - lowest)], sum_send.at[k])


def body(records, pair_list, live_count):
    tables = [jnp.asarray(table) for table in basis_tables()]
    any_space = pl.BlockSpec(memory_space=pl.ANY)
    vmem, bf16, f32 = pltpu.VMEM, jnp.bfloat16, jnp.float32
    dma = pltpu.SemaphoreType.DMA
    block_a = vmem((SIDE, SIDE, SEG, ROWS, CH), bf16)
    block_b = vmem((QUADS, OWNERS, 2, ROWS, CH), bf16)
    parts = vmem((TILES, SIDE * SEG * ROWS, TILE), f32)
    return pl.pallas_call(
        kernel,
        out_shape=vmem((2, 2 * BINS, PAIRS), f32),
        in_specs=[any_space] * 5,
        out_specs=pl.BlockSpec(memory_space=vmem),
        scratch_shapes=[
            vmem((2, SIDE, SIDE, ROWS, SAMPLES), bf16),
            vmem((SEG, SAMPLES, CH), bf16),
            vmem((2, PAIRS), jnp.int32),
            pltpu.SMEM((1,), jnp.int32),
            vmem((TILES, CH, TILE), bf16),
            vmem((TILES, 3 * CH, TILE), bf16),
            block_a,
            block_a,
            block_a,
            block_b,
            block_b,
            block_b,
            block_b,
            parts,
            parts,
            vmem((ROWS, PAIRS), f32),
            vmem((SIDE, SIDE, ROWS, PAIRS), bf16),
            vmem((SIDE, SIDE, ROWS, PAIRS), bf16),
            vmem((ROWS, PAIRS), f32),
            dma((4 + QUADS,)),
            dma((2, QUADS * EARLY + SIDE - EARLY)),
            dma((2, QUADS * EARLY + SIDE - EARLY)),
            dma((2, QUADS)),
            dma((2, QUADS)),
            dma((QUADS,)),
            dma((QUADS,)),
            dma((SIDE,)),
            dma((SIDE,)),
        ],
        compiler_params=pltpu.CompilerParams(
            collective_id=0, has_side_effects=True, vmem_limit_bytes=56 * 2**20
        ),
        cost_estimate=pl.CostEstimate(
            flops=7 * 10**9, bytes_accessed=4 * 2**20, transcendentals=0
        ),
    )(*tables, records, pair_list, live_count)


def solution(mesh):
    in_specs = (P("tm", None, "chan"), P(None, "chan"), P("chan"))
    out_specs = P(None, "tm", "chan")
    return jax.shard_map(body, mesh=mesh, in_specs=in_specs, out_specs=out_specs, check_vma=False)
```

```python
import functools
import math

import jax
import jax.numpy as jnp
import ml_dtypes
import numpy as np
from jax import lax
from jax.experimental import pallas as pl
from jax.experimental.pallas import tpu as pltpu
from jax.sharding import PartitionSpec as P

SAMPLES = 1024
NF = 256
BAND_LO = 16
EPSILON = 1e-06

SIDE = 4
OWNERS = SIDE * SIDE
SEG = 8
CH = 128
PAIRS = 1024
BINS = 8
ROWS = 2 * BINS
TILE = 256
TILES = PAIRS // TILE
QUADS = SEG // 2
EARLY = 2
MESH = pl.DeviceIdType.MESH


def basis_tables():
    sample_ids = np.arange(SAMPLES, dtype=np.int64)
    bin_ids = np.arange(NF, dtype=np.int64) + BAND_LO
    phases = bin_ids[:, None] * sample_ids[None, :] % SAMPLES
    step = np.float32(2.0 * math.pi / SAMPLES)
    angles = phases.astype(np.float32) * step
    tapers = np.float32(0.5) - np.float32(0.5) * np.cos(sample_ids.astype(np.float32) * step)
    table = np.stack([np.cos(angles) * tapers[None, :], -np.sin(angles) * tapers[None, :]])
    table = table.astype(np.float32).astype(ml_dtypes.bfloat16)
    table = table.reshape(2, SIDE, SIDE, 2, BINS, SAMPLES).transpose(3, 1, 2, 0, 4, 5)
    table = table.reshape(2, SIDE, SIDE, ROWS, SAMPLES)
    ids = np.arange(2 * SIDE - 1) % SIDE
    first = table[0][ids[None, :], (ids[:, None] + ids[None, :]) % SIDE]
    second = table[1][ids[:, None], ids[None, :]]
    return first, second


def kernel(
    basis_a_hbm, basis_b_hbm, rec_hbm, pair_hbm, live_hbm, out_ref,
    basis, rec, pair, live, w_left, w_right,
    own_a, near_a, far_a, stage_b, own_b, near_b, far_b, own_sum, send_sum, recv_sum, total_b,
    in_sem, za_send, za_recv, zb_send, zb_recv, gather_send, gather_recv, sum_send, sum_recv,
):
    t = lax.axis_index("tm")
    c = lax.axis_index("chan")
    n_chan = lax.axis_size("chan")
    y, x = lax.div(t, SIDE), lax.rem(t, SIDE)
    side = 1 - 2 * lax.rem(c, 2)
    c_near, c_far = c + side, c - side
    has_far = jnp.logical_and(c_far >= 0, c_far < n_chan)
    one_far = jnp.where(has_far, 1, 0)
    ways = ((0, near_a, near_b, c_near), (1, far_a, far_b, c_far))

    def on_way(way, act):
        if way == 0:
            act()
        else:
            pl.when(has_far)(act)

    def peer(dy, dx):
        return (lax.rem(y + dy, SIDE) * SIDE + lax.rem(x + dx, SIDE), c)

    others = [(dy, dx) for dy in (2, 1, 3, 0) for dx in (2, 1, 3, 0) if (dy, dx) != (0, 0)]

    barrier = pltpu.get_barrier_semaphore()
    for to in [peer(dy, dx) for dy, dx in others] + [(t, c_near)]:
        pl.semaphore_signal(barrier, inc=1, device_id=to, device_id_type=MESH)

    @pl.when(has_far)
    def _():
        pl.semaphore_signal(barrier, inc=1, device_id=(t, c_far), device_id_type=MESH)

    skew = lax.rem(x - y + SIDE, SIDE)
    basis_copies = [
        pltpu.make_async_copy(table.at[pl.ds(u, SIDE), pl.ds(v, SIDE)], basis.at[h], in_sem.at[2 + h])
        for h, (table, u, v) in enumerate(((basis_a_hbm, skew, y), (basis_b_hbm, y, x)))
    ]
    rec_copies = [
        pltpu.make_async_copy(rec_hbm.at[pl.ds(2 * q, 2)], rec.at[pl.ds(2 * q, 2)], in_sem.at[4 + q])
        for q in range(QUADS)
    ]
    pair_copy = pltpu.make_async_copy(pair_hbm, pair, in_sem.at[0])
    live_copy = pltpu.make_async_copy(live_hbm, live, in_sem.at[1])
    rec_copies[0].start()
    for copy in basis_copies:
        copy.start()
    for q in range(1, QUADS):
        rec_copies[q].start()
    pair_copy.start()
    live_copy.start()

    @pl.when(jnp.logical_not(has_far))
    def _():
        far_a[...] = jnp.zeros_like(far_a)
        far_b[...] = jnp.zeros_like(far_b)

    def make(source, landing, send_sem, recv_sem, to):
        return pltpu.make_async_remote_copy(
            src_ref=source,
            dst_ref=landing,
            send_sem=send_sem,
            recv_sem=recv_sem,
            device_id=to,
            device_id_type=MESH,
        )

    za, zb = [], []

    def send_z(copies, started=za):
        started.extend(copies)
        for way in (1, 0):
            @functools.partial(on_way, way)
            def _():
                for _, w, copy in copies:
                    if w == way:
                        copy.start()

    def wait_z(k, started=za):
        for way in range(2):
            @functools.partial(on_way, way)
            def _():
                for part, w, copy in started:
                    if part == k and w == way:
                        copy.wait()

    for copy in basis_copies:
        copy.wait()
    for q in range(QUADS):
        rec_copies[q].wait()
        wide = jnp.concatenate([rec[2 * q], rec[2 * q + 1]], axis=1)
        spectrum = jnp.dot(
            basis[...].reshape(2 * NF, SAMPLES), wide, preferred_element_type=jnp.float32
        )
        powers = jnp.sum(spectrum * spectrum, axis=0, keepdims=True) / NF
        white = (spectrum * lax.rsqrt(powers + EPSILON)).astype(jnp.bfloat16)
        for e in range(2):
            mine = white[:, e * CH:(e + 1) * CH].reshape(2, OWNERS, ROWS, CH)
            own_a[:, :, 2 * q + e] = mine[0].reshape(SIDE, SIDE, ROWS, CH)
            stage_b[q, :, e] = mine[1]
            own_b[q, 0, e] = mine[1, 0]
        if q == 0:
            pl.semaphore_wait(barrier, 1 + one_far + len(others))
        for k in range(EARLY):
            piece = (k, pl.ds(0, SIDE), pl.ds(2 * q, 2))
            sem = k * QUADS + q
            send_z([
                (k, way, make(own_a.at[piece], landing.at[piece], za_send.at[way, sem], za_recv.at[way, sem], (t, to)))
                for way, landing, _, to in ways
            ])
        for dy, dx in others:
            d = dy * SIDE + dx
            make(
                stage_b.at[q, d], own_b.at[q, d], gather_send.at[q], gather_recv.at[q], peer(dy, dx)
            ).start()
    for k in range(EARLY, SIDE):
        sem = QUADS * EARLY + k - EARLY
        send_z([
            (k, way, make(own_a.at[k], landing.at[k], za_send.at[way, sem], za_recv.at[way, sem], (t, to)))
            for way, landing, _, to in ways
        ])

    pair_copy.wait()
    live_copy.wait()
    n_live = live[0]
    for n in range(TILES):
        cols = pl.ds(n * TILE, TILE)
        left = pair[0:1, cols] - c * CH
        right = pair[1:2, cols] - (c - 1) * CH
        slots = lax.broadcasted_iota(jnp.int32, (1, TILE), 1) + n * TILE
        left = jnp.where(slots < n_live, left, -1)
        ids = lax.broadcasted_iota(jnp.int32, (CH, TILE), 0)
        w_left[n] = jnp.where(ids == left, 1.0 / 128.0, 0.0).astype(jnp.bfloat16)
        for place, block in ((0, 1), (1, 1 + side), (2, 1 - side)):
            hot = jnp.where(ids + block * CH == right, 1.0, 0.0)
            w_right[n, pl.ds(place * CH, CH)] = hot.astype(jnp.bfloat16)

    def multiply(own, near, far, groups):
        mine = own.reshape(-1, CH)
        wide = jnp.concatenate([mine, near.reshape(-1, CH), far.reshape(-1, CH)], axis=1)
        shape = (groups, mine.shape[0] // (groups * ROWS), 2, BINS, TILE)
        sums = []
        for n in range(TILES):
            left = jnp.dot(mine, w_left[n], preferred_element_type=jnp.float32).reshape(shape)
            right = jnp.dot(wide, w_right[n], preferred_element_type=jnp.float32).reshape(shape)
            real = jnp.sum(left[:, :, 0] * right[:, :, 0] + left[:, :, 1] * right[:, :, 1], axis=1)
            imag = jnp.sum(left[:, :, 1] * right[:, :, 0] - left[:, :, 0] * right[:, :, 1], axis=1)
            sums.append(jnp.concatenate([real, imag], axis=1))
        return sums

    def tile(n):
        return pl.ds(n * TILE, TILE)

    def part_a(k):
        wait_z(k)
        for n, both in enumerate(multiply(own_a[k], near_a[k], far_a[k], SIDE)):
            if k == 0:
                own_sum[:, tile(n)] = both[0]
            send_sum[k, :, :, tile(n)] = both.astype(jnp.bfloat16)
        for i in range(SIDE):
            dx = (i + k) % SIDE
            if (i, dx) != (0, 0):
                make(
                    send_sum.at[k, i], recv_sum.at[k, i], sum_send.at[k], sum_recv.at[k], peer(i, dx)
                ).start()

    def wait_bytes(ref, sem):
        pltpu.make_async_copy(ref, ref, sem).wait()

    def forward_b(q):
        wait_bytes(own_b.at[q, pl.ds(1, OWNERS - 1)], gather_recv.at[q])
        send_z([
            (q, way, make(own_b.at[q], landing.at[q], zb_send.at[way, q], zb_recv.at[way, q], (t, to)))
            for way, _, landing, to in ways
        ], zb)

    def part_b(q):
        wait_z(q, zb)
        for n, both in enumerate(multiply(own_b[q], near_b[q], far_b[q], 1)):
            if q == 0:
                total_b[:, tile(n)] = both[0]
            elif q < QUADS - 1:
                total_b[:, tile(n)] += both[0]
            else:
                total = total_b[:, tile(n)] + both[0]
                out_ref[0, BINS:, tile(n)] = total[:BINS]
                out_ref[1, BINS:, tile(n)] = total[BINS:]

    def add_sums(k):
        lowest = 1 if k == 0 else 0
        wait_bytes(recv_sum.at[k, pl.ds(lowest, SIDE - lowest)], sum_recv.at[k])
        total = own_sum[...]
        for i in range(lowest, SIDE):
            total = total + recv_sum[k, i].astype(jnp.float32)
        if k < SIDE - 1:
            own_sum[...] = total
        else:
            out_ref[0, :BINS] = total[:BINS]
            out_ref[1, :BINS] = total[BINS:]

    for k in range(SIDE):
        forward_b(k)
        part_a(k)
    part_b(0)
    part_b(1)
    add_sums(0)
    add_sums(1)
    part_b(2)
    add_sums(2)
    part_b(3)
    add_sums(3)
    for q in range(QUADS):
        wait_bytes(stage_b.at[q, pl.ds(1, OWNERS - 1)], gather_send.at[q])
    for k in range(SIDE):
        lowest = 1 if k == 0 else 0
        wait_bytes(send_sum.at[k, pl.ds(lowest, SIDE - lowest)], sum_send.at[k])


def body(records, pair_list, live_count):
    tables = [jnp.asarray(table) for table in basis_tables()]
    any_space = pl.BlockSpec(memory_space=pl.ANY)
    vmem, bf16, f32 = pltpu.VMEM, jnp.bfloat16, jnp.float32
    dma = pltpu.SemaphoreType.DMA
    block_a = vmem((SIDE, SIDE, SEG, ROWS, CH), bf16)
    block_b = vmem((QUADS, OWNERS, 2, ROWS, CH), bf16)
    return pl.pallas_call(
        kernel,
        out_shape=vmem((2, 2 * BINS, PAIRS), f32),
        in_specs=[any_space] * 5,
        out_specs=pl.BlockSpec(memory_space=vmem),
        scratch_shapes=[
            vmem((2, SIDE, SIDE, ROWS, SAMPLES), bf16),
            vmem((SEG, SAMPLES, CH), bf16),
            vmem((2, PAIRS), jnp.int32),
            pltpu.SMEM((1,), jnp.int32),
            vmem((TILES, CH, TILE), bf16),
            vmem((TILES, 3 * CH, TILE), bf16),
            block_a,
            block_a,
            block_a,
            block_b,
            block_b,
            block_b,
            block_b,
            vmem((ROWS, PAIRS), f32),
            vmem((SIDE, SIDE, ROWS, PAIRS), bf16),
            vmem((SIDE, SIDE, ROWS, PAIRS), bf16),
            vmem((ROWS, PAIRS), f32),
            dma((4 + QUADS,)),
            dma((2, QUADS * EARLY + SIDE - EARLY)),
            dma((2, QUADS * EARLY + SIDE - EARLY)),
            dma((2, QUADS)),
            dma((2, QUADS)),
            dma((QUADS,)),
            dma((QUADS,)),
            dma((SIDE,)),
            dma((SIDE,)),
        ],
        compiler_params=pltpu.CompilerParams(
            collective_id=0, has_side_effects=True, vmem_limit_bytes=56 * 2**20
        ),
        cost_estimate=pl.CostEstimate(
            flops=7 * 10**9, bytes_accessed=4 * 2**20, transcendentals=0
        ),
    )(*tables, records, pair_list, live_count)


def solution(mesh):
    in_specs = (P("tm", None, "chan"), P(None, "chan"), P("chan"))
    out_specs = P(None, "tm", "chan")
    return jax.shard_map(body, mesh=mesh, in_specs=in_specs, out_specs=out_specs, check_vma=False)
```
